128 devices in a mesh: seq: 32 (over x, y_hi, z), tensor: 4 (over y_lo, core).
Axes of the slice: x: 4, y: 4 (y_hi: 2, y_lo: 2; y = y_hi * 2 + y_lo), z: 4, core: 2. Of those that a mesh axis runs over, the one named last changes fastest.
Arguments:
- states_forward: bfloat16 [32768, 8192], P(('seq', 'tensor')), may hold values from -6 to 6
- norm_gain: bfloat16 [8192], replicated, may hold values from 0.25 to 1.75
- query_weight: bfloat16 [8192, 4096], P('seq', 'tensor')
- frozen_key_weight: bfloat16 [8192, 512], P('seq', 'tensor')
- frozen_value_weight: bfloat16 [8192, 512], P('seq', 'tensor'), may hold values from -0.0625 to 0.0625
- query_down: bfloat16 [8192, 16], replicated, may hold values from -0.0625 to 0.0625
- query_up: bfloat16 [16, 4096], P(None, 'tensor'), may hold values from -0.75 to 0.75
- key_down_matrix: bfloat16 [8192, 16], replicated, may hold values from -0.0625 to 0.0625
- key_up_matrix: bfloat16 [16, 512], P(None, 'tensor'), may hold values from -0.75 to 0.75
- value_down_matrix: bfloat16 [8192, 16], replicated, may hold values from -0.0625 to 0.0625
- value_up_matrix: bfloat16 [16, 512], P(None, 'tensor'), may hold values from -0.75 to 0.75
- shifted: int32 [4], P('tensor'), may hold values from 0 to 1, as said below
- saved_context: bfloat16 [32768, 4096], P('seq', 'tensor'), may hold values from -6 to 6
- output_gradient: bfloat16 [32768, 8192], P(('seq', 'tensor')), may hold values from -0.032958984 to 0.032958984
- out_down: bfloat16 [4096, 16], P('tensor'), may hold values from -0.09375 to 0.09375
- out_up: bfloat16 [16, 8192], replicated, may hold values from -1.5 to 1.5
Outputs:
- context_forward: bfloat16 [32768, 4096], P('seq', 'tensor')
- down_output_gradient: float32 [4096, 16], P('tensor')
- up_output_gradient: float32 [16, 8192], replicated
The draws below stay inside these ranges and needn't reach their ends.
Inputs may be any that keep to these rules, and one draw needn't show every extreme that they name: `shifted`: exactly 2 entries are 1; which ones is drawn.
All inputs are finite; a program needn't handle non-finite values.
Results may differ from the reference program's by a relative error of at most 0.012.
The reference program's roundings to bfloat16 on the way count: a program that leaves them out, or rounds other values in their place, can miss the bound.
Values may be sent and summed in bfloat16 or wider, within the bound.
A program may use at most 192 MiB of HBM per device.

```python
import math
import jax
import jax.numpy as jnp
from jax import lax

MODEL_WIDTH = 8192
HEAD_WIDTH = 128
QUERY_HEADS = 32
KEY_VALUE_HEADS = 4
ADAPTER_RANK = 16
GROUP = 2048
BLK = 1024
SEQUENCE_TOKENS = 32768


def key_matrix(key):
    return jnp.clip(jax.random.normal(key, (MODEL_WIDTH, KEY_VALUE_HEADS * HEAD_WIDTH), jnp.float32), -5.0, 5.0) / math.sqrt(MODEL_WIDTH)


def draw_frozen_key_weight(key, part):
    return key_matrix(key).astype(jnp.bfloat16)


def draw_query_weight(key, part):
    key = jax.random.fold_in(key, 11)
    noise = jnp.clip(jax.random.normal(jax.random.fold_in(key, 1), (MODEL_WIDTH, QUERY_HEADS * HEAD_WIDTH), jnp.float32), -5.0, 5.0) / math.sqrt(MODEL_WIDTH)
    return noise.astype(jnp.bfloat16)


def draw_shifted(key, part):
    key = jax.random.fold_in(key, 5)
    sorting_order = jax.random.permutation(key, KEY_VALUE_HEADS)
    return (sorting_order < KEY_VALUE_HEADS // 2).astype(jnp.int32)


def levels(stream_key, shape, split, smallest, high):
    factor_of = 1.0
    for axis_at, shards_of in split:
        steps = jax.random.uniform(jax.random.fold_in(jax.random.fold_in(stream_key, 6), axis_at), (shards_of,), jnp.float32, smallest / len(split), high / len(split))
        factor_of = factor_of * jnp.repeat(jnp.exp(steps), shape[axis_at] // shards_of).reshape((-1,) + (1,) * (len(shape) - 1 - axis_at))
    return factor_of


def scatter_about(own_key, extent, spread, most, shards=(), held_as=jnp.bfloat16):
    level = levels(own_key, extent, shards, -0.22, 0.18) if shards else 1.0
    entries = jax.random.normal(own_key, extent, jnp.float32) * spread * level
    return jnp.minimum(jnp.maximum(entries, -most), most).astype(held_as)


def setup_inputs(seed: int = 0) -> dict:
    arg_keys = jax.random.split(jax.random.key(seed), 17)
    states_forward = scatter_about(arg_keys[0], (SEQUENCE_TOKENS, MODEL_WIDTH), 1.0, 6.0, ((0, 128),))
    norm_gain = jnp.clip(1.0 + 0.15 * jax.random.normal(arg_keys[1], (MODEL_WIDTH,), jnp.float32), 0.25, 1.75).astype(jnp.bfloat16)
    query_weight = draw_query_weight(jax.random.fold_in(arg_keys[16], 71), 0)
    frozen_key_weight = draw_frozen_key_weight(jax.random.fold_in(arg_keys[16], 71), 0)
    frozen_value_weight = scatter_about(arg_keys[4], (MODEL_WIDTH, KEY_VALUE_HEADS * HEAD_WIDTH), MODEL_WIDTH ** -0.5, 0.0625, ((0, 32), (1, 4)))
    query_down = scatter_about(arg_keys[5], (MODEL_WIDTH, ADAPTER_RANK), MODEL_WIDTH ** -0.5, 0.0625)
    query_up = scatter_about(arg_keys[6], (ADAPTER_RANK, QUERY_HEADS * HEAD_WIDTH), (4 * ADAPTER_RANK) ** -0.5, 0.75, ((1, 4),))
    key_down_matrix = scatter_about(arg_keys[7], (MODEL_WIDTH, ADAPTER_RANK), MODEL_WIDTH ** -0.5, 0.0625)
    key_up_matrix = scatter_about(arg_keys[8], (ADAPTER_RANK, KEY_VALUE_HEADS * HEAD_WIDTH), (4 * ADAPTER_RANK) ** -0.5, 0.75, ((1, 4),))
    value_down_matrix = scatter_about(arg_keys[9], (MODEL_WIDTH, ADAPTER_RANK), MODEL_WIDTH ** -0.5, 0.0625)
    value_up_matrix = scatter_about(arg_keys[10], (ADAPTER_RANK, KEY_VALUE_HEADS * HEAD_WIDTH), (4 * ADAPTER_RANK) ** -0.5, 0.75, ((1, 4),))
    shifted = draw_shifted(jax.random.fold_in(arg_keys[16], 71), 0)
    saved_context = scatter_about(arg_keys[12], (SEQUENCE_TOKENS, QUERY_HEADS * HEAD_WIDTH), 1.0, 6.0, ((0, 32), (1, 4)))
    output_gradient = scatter_about(arg_keys[13], (SEQUENCE_TOKENS, MODEL_WIDTH), (SEQUENCE_TOKENS ** -0.5), 0.032958984, ((0, 128),))
    out_down = scatter_about(arg_keys[14], (QUERY_HEADS * HEAD_WIDTH, ADAPTER_RANK), (QUERY_HEADS * HEAD_WIDTH) ** -0.5, 0.09375, ((0, 4),))
    out_up = scatter_about(arg_keys[15], (ADAPTER_RANK, MODEL_WIDTH), ADAPTER_RANK ** -0.5, 1.5)
    return dict(states_forward=states_forward, norm_gain=norm_gain, query_weight=query_weight, frozen_key_weight=frozen_key_weight, frozen_value_weight=frozen_value_weight, query_down=query_down, query_up=query_up, key_down_matrix=key_down_matrix, key_up_matrix=key_up_matrix, value_down_matrix=value_down_matrix, value_up_matrix=value_up_matrix, shifted=shifted, saved_context=saved_context, output_gradient=output_gradient, out_down=out_down, out_up=out_up)


EPS = 1e-05
ADAPTER_SCALE = 2.0
ROPE_STRETCH = 0.125

def normalize(states, gain):
    wide = states.astype(jnp.float32)
    factor = lax.rsqrt(lax.optimization_barrier(jnp.mean(wide * wide, axis=-1, keepdims=True)) + EPS)
    return (wide * factor * gain.astype(jnp.float32)).astype(jnp.bfloat16)

def apply_rotation(vectors, token_positions):
    half = vectors.shape[-1] // 2
    index = jnp.arange(half).astype(jnp.float32)
    inverse = jnp.exp(index * (-2.0 * math.log(10000.0) / vectors.shape[-1]))
    angle = (token_positions.astype(jnp.float32) * ROPE_STRETCH)[:, None] * inverse[None, :]
    cosine = jnp.cos(angle)[:, None, :]
    sine = jnp.sin(angle)[:, None, :]
    first = vectors[..., :half]
    second = vectors[..., half:]
    return jnp.concatenate([first * cosine - second * sine, second * cosine + first * sine], axis=-1)

def apply_projection(normalized_input, weight, down, up_matrix):
    reduced_result = jnp.dot(normalized_input, down, preferred_element_type=jnp.float32).astype(jnp.bfloat16)
    frozen_part = jnp.dot(normalized_input, weight, preferred_element_type=jnp.float32)
    return frozen_part + ADAPTER_SCALE * jnp.dot(reduced_result, up_matrix, preferred_element_type=jnp.float32)

def group_attention(operands):
    query_tensor, key_tensor, value_tensor = operands
    head_size = key_tensor.shape[-1]
    scores = jnp.einsum('qhd,kd->hqk', query_tensor.astype(jnp.float32), key_tensor.astype(jnp.float32)) / math.sqrt(head_size)
    length = key_tensor.shape[0]
    causal = jnp.arange(length)[:, None] >= jnp.arange(length)[None, :]
    scores = jnp.where(causal[None], scores, -jnp.inf)
    summit = lax.optimization_barrier(jnp.max(scores, axis=-1, keepdims=True))
    raised = jnp.exp(scores - summit)
    shares = (raised / lax.optimization_barrier(jnp.sum(raised, axis=-1, keepdims=True))).astype(jnp.bfloat16)
    return jnp.einsum('hqk,kd->qhd', shares.astype(jnp.float32), value_tensor.astype(jnp.float32))

def reference(states_forward, norm_gain, query_weight, frozen_key_weight, frozen_value_weight, query_down, query_up, key_down_matrix, key_up_matrix, value_down_matrix, value_up_matrix, shifted, saved_context, output_gradient, out_down, out_up):
    normalized_input = normalize(states_forward, norm_gain)
    token_positions = jnp.arange(SEQUENCE_TOKENS).astype(jnp.int32)
    group_ratio = QUERY_HEADS // KEY_VALUE_HEADS
    query_tensor = apply_rotation(apply_projection(normalized_input, query_weight, query_down, query_up).reshape(SEQUENCE_TOKENS, QUERY_HEADS, HEAD_WIDTH), token_positions).astype(jnp.bfloat16)
    key_tensor = apply_rotation(apply_projection(normalized_input, frozen_key_weight, key_down_matrix, key_up_matrix).reshape(SEQUENCE_TOKENS, KEY_VALUE_HEADS, HEAD_WIDTH), token_positions).astype(jnp.bfloat16)
    value_tensor = apply_projection(normalized_input, frozen_value_weight, value_down_matrix, value_up_matrix).reshape(SEQUENCE_TOKENS, KEY_VALUE_HEADS, HEAD_WIDTH).astype(jnp.bfloat16)
    query_tensor = query_tensor.reshape(SEQUENCE_TOKENS, KEY_VALUE_HEADS, group_ratio, HEAD_WIDTH)
    groups = SEQUENCE_TOKENS // GROUP

    def one_kv_head(operands):
        query_head, key_head, value_head, flag = operands
        moved = flag == 1
        query_head = jnp.where(moved, jnp.roll(query_head, -BLK, axis=0), query_head)
        key_head = jnp.where(moved, jnp.roll(key_head, -BLK, axis=0), key_head)
        value_head = jnp.where(moved, jnp.roll(value_head, -BLK, axis=0), value_head)
        outcome = lax.map(group_attention, (query_head.reshape(groups, GROUP, group_ratio, HEAD_WIDTH), key_head.reshape(groups, GROUP, HEAD_WIDTH), value_head.reshape(groups, GROUP, HEAD_WIDTH)))
        outcome = outcome.reshape(SEQUENCE_TOKENS, group_ratio, HEAD_WIDTH)
        return jnp.where(moved, jnp.roll(outcome, BLK, axis=0), outcome)
    heads_out = lax.map(one_kv_head, (jnp.moveaxis(query_tensor, 1, 0), jnp.moveaxis(key_tensor, 1, 0), jnp.moveaxis(value_tensor, 1, 0), shifted))
    context_forward = jnp.moveaxis(heads_out, 0, 1).reshape(SEQUENCE_TOKENS, QUERY_HEADS * HEAD_WIDTH).astype(jnp.bfloat16)
    reduced_gradient = jnp.dot(output_gradient, out_up.T, preferred_element_type=jnp.float32).astype(jnp.bfloat16)
    reduced_context = jnp.dot(saved_context, out_down, preferred_element_type=jnp.float32).astype(jnp.bfloat16)
    down_output_gradient = ADAPTER_SCALE * jnp.dot(saved_context.T, reduced_gradient, preferred_element_type=jnp.float32)
    up_output_gradient = ADAPTER_SCALE * jnp.dot(reduced_context.T, output_gradient, preferred_element_type=jnp.float32)
    return (context_forward, down_output_gradient, up_output_gradient)
```

```python
import math

import jax
import jax.numpy as jnp
from jax import lax
from jax.experimental import pallas as pl
from jax.experimental.pallas import tpu as pltpu
from jax.sharding import PartitionSpec as P

HEAD = 128
EPS = 1e-05
ADAPTER_SCALE = 2.0
ROPE_STRETCH = 0.125
BLOCK = 1024
OWN = 256
PIECE = 256
PIECES = 32
COLS = 1280
HEADS = 8
NT = (((1,), (1,)), ((), ()))
MESH = pl.DeviceIdType.MESH

ORDER = [
    (0, 0, 0),
    (0, 3, 0), (0, 1, 0), (0, 0, 3), (0, 0, 1),
    (1, 0, 0),
    (0, 2, 0), (0, 0, 2),
    (1, 3, 0), (1, 1, 0), (1, 0, 3), (1, 0, 1),
    (1, 2, 0), (1, 0, 2),
    (1, 3, 3), (1, 1, 3), (0, 3, 3), (0, 3, 1),
    (1, 2, 3), (0, 3, 2),
    (1, 3, 1), (1, 1, 1), (0, 1, 3), (0, 1, 1),
    (1, 2, 1), (0, 1, 2),
    (1, 3, 2), (1, 1, 2), (0, 2, 3), (0, 2, 1),
    (1, 2, 2), (0, 2, 2),
]
SLOT = {piece: at for at, piece in enumerate(ORDER)}
GROUPS = 8
SPAN = PIECES // GROUPS


def f32_dot(a, b, dims=(((1,), (0,)), ((), ()))):
    return lax.dot_general(a, b, dims, preferred_element_type=jnp.float32)


def project(
    states, gain, wq, wk, wv, downs_q, downs_k, downs_v, up_q, up_k, up_v, saved, grad, odown, oup,
    q_out, kv_out, dgrad, ugrad,
    w, nb, acc, big, sc, dn_cat, up_cat, low, cos_t, sin_t, oup_v, od_v,
    lg, part, part_r1, part_r2, ctx, up, up_r3, up_r4, up_r5, up_r6, up_r7, up_r8, up_r9, up_t,
    dn, dn_r5, dn_r6, dn_r7, dn_r8, dn_r9, dn_t, up_g, dn_g,
    local, w_send, w_recv, n_send, n_recv, g_send, g_recv,
):
    s = lax.axis_index("seq")
    t = lax.axis_index("tensor")
    z = s % 4
    yh = (s // 4) % 2
    x = s // 8
    yl = t // 2
    core = t % 2

    def dev(x=x, yh=yh, z=z, yl=yl, core=core):
        return ((x * 2 + yh) * 4 + z, yl * 2 + core)

    side = {
        ("x", 1): dev(x=(x + 1) % 4),
        ("x", -1): dev(x=(x + 3) % 4),
        ("z", 1): dev(z=(z + 1) % 4),
        ("z", -1): dev(z=(z + 3) % 4),
    }
    p_core = dev(core=1 - core)
    p_yl = dev(yl=1 - yl)
    p_yh = dev(yh=1 - yh)
    p_x1 = dev(x=x + 1 - 2 * (x % 2))
    p_x2 = dev(x=3 - x)
    p_z1 = dev(z=z + 1 - 2 * (z % 2))
    p_z2 = dev(z=3 - z)
    later = ((s + 1) % 32, t)
    before = ((s + 31) % 32, t)

    def local_copy(src, dst, at):
        return pltpu.make_async_copy(src, dst, local.at[at])

    own_w = [
        local_copy(wq, w.at[0, :, 0:1024], 0),
        local_copy(wk, w.at[0, :, 1024:1152], 1),
        local_copy(wv, w.at[0, :, 1152:1280], 2),
    ]
    for c in own_w:
        c.start()
    load_states = local_copy(states, big, 3)
    load_states.start()

    barrier = pltpu.get_barrier_semaphore()
    greeted = list(side.values()) + [p_core, p_yl, p_yh, later, before]
    for d in greeted:
        pl.semaphore_signal(barrier, inc=1, device_id=d, device_id_type=MESH)
    pl.semaphore_wait(barrier, len(greeted))

    sends = []

    def remote(src, dst, send, recv, to):
        c = pltpu.make_async_remote_copy(
            src_ref=src, dst_ref=dst, send_sem=send, recv_sem=recv, device_id=to, device_id_type=MESH
        )
        c.start()
        sends.append(c)
        return c

    arrivals = {}
    moves = []

    def move(piece, axis, way, half=None):
        o, rx, rz = piece
        at = {"x": rx, "z": rz}
        at[axis] = (at[axis] - way) % 4
        to = SLOT[(o, at["x"], at["z"])]
        frm = SLOT[piece]
        rows = slice(0, PIECE) if half is None else slice(half * 128, half * 128 + 128)
        moves.append(to)
        c = remote(
            w.at[frm, rows], w.at[to, rows], w_send.at[len(moves)], w_recv.at[to, half or 0], side[(axis, way)]
        )
        arrivals.setdefault(to, []).append(c)

    def pass_on(piece):
        o, rx, rz = piece
        first, second = ("x", "z") if o == 0 else ("z", "x")
        r1, r2 = (rx, rz) if o == 0 else (rz, rx)
        if r2 == 0:
            if r1 == 0:
                move(piece, first, 1)
                move(piece, first, -1)
            elif r1 == 3:
                move(piece, first, 1, 0)
            elif r1 == 1:
                move(piece, first, -1, 1)
            move(piece, second, 1)
            move(piece, second, -1)
        elif r2 == 3:
            move(piece, second, 1, 0)
        elif r2 == 1:
            move(piece, second, -1, 1)

    for c in own_w:
        c.wait()
    other = remote(w.at[0], w.at[SLOT[(1, 0, 0)]], w_send.at[0], w_recv.at[SLOT[(1, 0, 0)], 0], p_yh)
    pass_on((0, 0, 0))

    loads = [
        local_copy(downs_q, dn_cat.at[0:16], 4),
        local_copy(downs_k, dn_cat.at[16:32], 5),
        local_copy(downs_v, dn_cat.at[32:48], 6),
        local_copy(oup, oup_v, 10),
        local_copy(odown, od_v, 11),
        local_copy(saved, sc, 12),
    ]
    for c in loads:
        c.start()

    load_states.wait()

    def squares(c, total):
        at = pl.multiple_of(c * 256, 256)
        one = big[:, pl.ds(at, 128)].astype(jnp.float32)
        two = big[:, pl.ds(at + 128, 128)].astype(jnp.float32)
        return total + (one * one + two * two)

    total = lax.fori_loop(0, 32, squares, jnp.zeros((OWN, 128), jnp.float32))
    factor = lax.rsqrt(jnp.sum(total, axis=1, keepdims=True) / 8192.0 + EPS)

    def source(piece):
        o, rx, rz = piece
        return (((x + rx) % 4) * 2 + (yh + o) % 2) * 4 + (z + rz) % 4

    n_mine = []
    for g in range(GROUPS):
        for j in range(g * SPAN, (g + 1) * SPAN):
            at = pl.multiple_of(source(ORDER[j]) * PIECE, PIECE)
            wide = big[:, pl.ds(at, PIECE)].astype(jnp.float32)
            scale = gain[:, pl.ds(at, PIECE)].astype(jnp.float32)
            nb[t, j] = (wide * factor * scale).astype(jnp.bfloat16)
        cols = pl.ds(g * SPAN, SPAN)
        to_y = remote(nb.at[t, cols], nb.at[t, cols], n_send.at[0, g], n_recv.at[0, g], p_yl)
        to_core = remote(nb.at[t, cols], nb.at[t, cols], n_send.at[1, g], n_recv.at[1, g], p_core)
        n_mine.append((to_y, to_core))

    load_grad = local_copy(grad, big, 13)
    load_grad.start()
    for c in loads[:3]:
        c.wait()

    total = jnp.zeros((OWN, 48), jnp.float32)
    for j in range(PIECES):
        at = pl.multiple_of(source(ORDER[j]) * PIECE, PIECE)
        total = total + f32_dot(nb[t, j], dn_cat[:, pl.ds(at, PIECE)], NT)
    low[t, :, 0:48] = total.astype(jnp.bfloat16)
    low[t, :, 48:128] = jnp.zeros((OWN, 80), jnp.bfloat16)

    exchanges = {}

    def swap(at, src, dst, to):
        exchanges[at] = remote(src, dst, g_send.at[at], g_recv.at[at], to)

    def got(at):
        exchanges[at].wait_recv()

    up_cat[...] = jnp.zeros_like(up_cat)
    ups = [
        local_copy(up_q, up_cat.at[0:16, 0:1024], 7),
        local_copy(up_k, up_cat.at[16:32, 1024:1152], 8),
        local_copy(up_v, up_cat.at[32:48, 1152:1280], 9),
    ]
    for c in ups:
        c.start()

    lane = lax.broadcasted_iota(jnp.int32, (256, HEAD), 1)
    index = (lane % 64).astype(jnp.float32)
    inverse = jnp.exp(index * (-2.0 * math.log(10000.0) / HEAD))
    sign = jnp.where(lane < 64, -1.0, 1.0).astype(jnp.float32)

    def tables(i, carry):
        at = pl.multiple_of(i * 256, 256)
        position = lax.broadcasted_iota(jnp.int32, (256, HEAD), 0) + (s * BLOCK + at)
        angle = position.astype(jnp.float32) * ROPE_STRETCH * inverse
        cos_t[pl.ds(at, 256), :] = jnp.cos(angle)
        sin_t[pl.ds(at, 256), :] = jnp.sin(angle) * sign
        return carry

    for c in loads[3:]:
        c.wait()
    load_grad.wait()

    xa = (x + x // 2) % 2
    xb = x // 2
    u3, u4, u5, u6, u7 = (
        core * 16,
        core * 16 + yl * 8,
        core * 16 + yl * 8 + yh * 4,
        core * 16 + yl * 8 + yh * 4 + xa * 2,
        core * 16 + yl * 8 + yh * 4 + xa * 2 + xb,
    )
    v3 = (1 - core) * 16
    v4 = u3 + (1 - yl) * 8
    v5 = u4 + (1 - yh) * 4
    v6 = u5 + (1 - xa) * 2
    v7 = u6 + (1 - xb)
    d5, d6, d7 = yh * 4, yh * 4 + xa * 2, yh * 4 + xa * 2 + xb
    e5, e6, e7 = (1 - yh) * 4, d5 + (1 - xa) * 2, d6 + (1 - xb)

    def g0():
        swap(24, low.at[t], low.at[t], p_core)
        total = jnp.zeros((16, OWN), jnp.float32)
        for c in range(16):
            cols = slice(c * 512, c * 512 + 512)
            total = total + f32_dot(oup_v[:, cols], big[:, cols], NT)
        lg[t] = total.astype(jnp.bfloat16)
        swap(0, lg.at[t], lg.at[t], p_core)
        for b in range(4):
            part[b] = f32_dot(od_v[...], sc[b * 256 : b * 256 + 256, :], NT)
        swap(1, part.at[pl.ds((1 - yl) * 2, 2)], part_r1, p_yl)

    def g1():
        got(24)
        swap(25, low.at[pl.ds(yl * 2, 2)], low.at[pl.ds(yl * 2, 2)], p_yl)
        got(0)
        swap(2, lg.at[pl.ds(yl * 2, 2)], lg.at[pl.ds(yl * 2, 2)], p_yl)
        got(1)
        keep = pl.ds(yl * 2, 2)
        part[keep] = part[keep] + part_r1[...]
        swap(3, part.at[yl * 2 + 1 - core], part_r2, p_core)

    def g2():
        got(2)
        got(3)
        ctx[...] = (part[t] + part_r2[...]).astype(jnp.bfloat16)
        for b in range(8):
            sums = jnp.zeros((16, 128), jnp.float32)
            for k in range(4):
                sums = sums + f32_dot(lg[k], sc[k * 256 : k * 256 + 256, b * 128 : b * 128 + 128])
            dn[b] = ADAPTER_SCALE * sums
        for b in range(32):
            up[b] = ADAPTER_SCALE * f32_dot(ctx[...], big[:, b * 256 : b * 256 + 256])
        swap(4, up.at[pl.ds(v3, 16)], up_r3, p_core)

    def g3():
        got(4)
        up[pl.ds(u3, 16)] = up[pl.ds(u3, 16)] + up_r3[...]
        swap(5, up.at[pl.ds(v4, 8)], up_r4, p_yl)

    def g4():
        got(5)
        up[pl.ds(u4, 8)] = up[pl.ds(u4, 8)] + up_r4[...]
        swap(6, up.at[pl.ds(v5, 4)], up_r5, p_yh)
        swap(7, dn.at[pl.ds(e5, 4)], dn_r5, p_yh)

    def g5():
        got(6)
        got(7)
        up[pl.ds(u5, 4)] = up[pl.ds(u5, 4)] + up_r5[...]
        dn[pl.ds(d5, 4)] = dn[pl.ds(d5, 4)] + dn_r5[...]
        swap(8, up.at[pl.ds(v6, 2)], up_r6, p_x1)
        swap(9, dn.at[pl.ds(e6, 2)], dn_r6, p_x1)

    def g6():
        got(8)
        got(9)
        up[pl.ds(u6, 2)] = up[pl.ds(u6, 2)] + up_r6[...]
        dn[pl.ds(d6, 2)] = dn[pl.ds(d6, 2)] + dn_r6[...]
        swap(10, up.at[v7], up_r7, p_x2)
        swap(11, dn.at[e7], dn_r7, p_x2)

    def g7():
        got(10)
        got(11)
        up[u7] = up[u7] + up_r7[...]
        dn[d7] = dn[d7] + dn_r7[...]
        swap(12, up.at[u7], up_r8, p_z1)
        swap(13, dn.at[d7], dn_r8, p_z1)

    def g8():
        got(12)
        got(13)
        up_t[...] = up[u7] + up_r8[...]
        dn_t[...] = dn[d7] + dn_r8[...]
        swap(14, up_t, up_r9, p_z2)
        swap(15, dn_t, dn_r9, p_z2)

    def g9():
        got(14)
        got(15)
        up_g[u7] = up_t[...] + up_r9[...]
        dn_g[d7] = dn_t[...] + dn_r9[...]
        swap(16, up_g.at[u7], up_g.at[u7], p_x2)
        swap(17, dn_g.at[d7], dn_g.at[d7], p_x2)

    def g10():
        got(16)
        got(17)
        swap(18, up_g.at[pl.ds(u6, 2)], up_g.at[pl.ds(u6, 2)], p_x1)
        swap(19, dn_g.at[pl.ds(d6, 2)], dn_g.at[pl.ds(d6, 2)], p_x1)

    def g11():
        got(18)
        got(19)
        swap(20, up_g.at[pl.ds(u5, 4)], up_g.at[pl.ds(u5, 4)], p_yh)
        swap(21, dn_g.at[pl.ds(d5, 4)], dn_g.at[pl.ds(d5, 4)], p_yh)

    def g12():
        got(20)
        got(21)
        swap(22, up_g.at[pl.ds(u4, 8)], up_g.at[pl.ds(u4, 8)], p_yl)

    def g13():
        got(22)
        swap(23, up_g.at[pl.ds(u3, 16)], up_g.at[pl.ds(u3, 16)], p_core)

    def g14():
        got(23)
        for b in range(32):
            ugrad[:, b * 256 : b * 256 + 256] = up_g[b]
        for b in range(8):
            dgrad[:, b * 128 : b * 128 + 128] = dn_g[b]

    def adapter():
        got(25)
        for c in ups:
            c.wait()

        def rows_of(i, carry):
            rows = pl.ds(pl.multiple_of(i * 256, 256), 256)
            for c in range(5):
                cols = slice(c * 256, c * 256 + 256)
                acc[rows, cols] = ADAPTER_SCALE * f32_dot(low[i], up_cat[:, cols])
            return carry

        lax.fori_loop(0, 4, rows_of, 0)

    def multiply(ja, jb):
        def rows_of(i, carry):
            rows = pl.ds(pl.multiple_of(i * 256, 256), 256)
            for c in range(5):
                cols = slice(c * 256, c * 256 + 256)
                acc[rows, cols] += f32_dot(nb[i, ja], w[ja, :, cols]) + f32_dot(nb[i, jb], w[jb, :, cols])
            return carry

        lax.fori_loop(0, 4, rows_of, 0)

    hooks = {
        0: [g0, lambda: lax.fori_loop(0, 4, tables, 0)],
        1: [g1],
        2: [g2],
        3: [adapter, g3],
        5: [g4],
        7: [g5],
        9: [g6],
        11: [g7],
        13: [g8],
        15: [g9],
        17: [g10],
        19: [g11],
        21: [g12],
        23: [g13],
        25: [g14],
    }
    arrivals[SLOT[(1, 0, 0)]] = [other]
    for j in range(PIECES):
        if j > 0:
            for c in arrivals[j]:
                c.wait_recv()
            pass_on(ORDER[j])
        if j % SPAN == SPAN - 1:
            g = j // SPAN
            n_mine[g][0].wait_recv()
            cols = pl.ds(g * SPAN, SPAN)
            theirs = (1 - yl) * 2 + core
            fwd = remote(
                nb.at[theirs, cols], nb.at[theirs, cols], n_send.at[2, g], n_recv.at[2, g], p_core
            )
        for f in hooks.get(j, []):
            f()
        if j % SPAN == SPAN - 1:
            n_mine[g][1].wait_recv()
            fwd.wait_recv()
            for k in range(j - SPAN + 1, j + 1, 2):
                multiply(k, k + 1)

    def rotated(value, rows):
        return value * cos_t[rows, :] + pltpu.roll(value, 64, 1) * sin_t[rows, :]

    def keys_of(i, carry):
        at = pl.multiple_of(i * 256, 256)
        rows = pl.ds(at, 256)
        kv_out[0, pl.ds(BLOCK + at, 256), :] = rotated(acc[rows, 1024:1152], rows).astype(jnp.bfloat16)
        kv_out[1, pl.ds(BLOCK + at, 256), :] = acc[rows, 1152:1280].astype(jnp.bfloat16)
        return carry

    lax.fori_loop(0, 4, keys_of, 0)
    mine = pl.ds(BLOCK, BLOCK)
    prior = remote(kv_out.at[:, mine], kv_out.at[:, pl.ds(0, BLOCK)], g_send.at[26], g_recv.at[26], later)

    def queries_of(i, carry):
        rows = pl.ds(pl.multiple_of(i * 256, 256), 256)
        for h in range(HEADS):
            cols = slice(h * HEAD, h * HEAD + HEAD)
            q_out[rows, cols] = rotated(acc[rows, cols], rows).astype(jnp.bfloat16)
        return carry

    lax.fori_loop(0, 4, queries_of, 0)
    prior.wait_recv()
    for c in sends:
        c.wait_send()


def attend(flag, q, k, v, out):
    contract = 1.4426950408889634 / math.sqrt(HEAD)

    def tile(i, start):
        rows = slice(i * 256, i * 256 + 256)
        stop = BLOCK + (i + 1) * 256
        scores = f32_dot(q[rows, :], k[start:stop, :], NT)
        width = stop - start
        key = lax.broadcasted_iota(jnp.int32, (256, 256), 1)
        query = lax.broadcasted_iota(jnp.int32, (256, 256), 0)
        corner = jnp.where(key <= query, scores[:, width - 256 :], -jnp.inf)
        if width > 256:
            scores = jnp.concatenate([scores[:, : width - 256], corner], axis=1)
        else:
            scores = corner
        summit = jnp.max(scores, axis=1, keepdims=True)
        raised = jnp.exp2((scores - summit) * contract)
        norm = jnp.sum(raised, axis=1, keepdims=True)
        found = f32_dot(raised.astype(jnp.bfloat16), v[start:stop, :])
        out[rows, :] = (found / norm).astype(jnp.bfloat16)

    @pl.when(flag[0] == 1)
    def _():
        for i in range(4):
            tile(i, 0)

    @pl.when(flag[0] == 0)
    def _():
        for i in range(4):
            tile(i, BLOCK)


def on_device(
    states_forward, norm_gain, query_weight, frozen_key_weight, frozen_value_weight, query_down, query_up,
    key_down_matrix, key_up_matrix, value_down_matrix, value_up_matrix, shifted, saved_context, output_gradient,
    out_down, out_up,
):
    bf16, f32 = jnp.bfloat16, jnp.float32
    hbm = pl.BlockSpec(memory_space=pl.ANY)
    vmem = pl.BlockSpec(memory_space=pltpu.VMEM)
    scratch = [
        pltpu.VMEM((PIECES, PIECE, COLS), bf16),
        pltpu.VMEM((4, PIECES, OWN, PIECE), bf16),
        pltpu.VMEM((BLOCK, COLS), f32),
        pltpu.VMEM((OWN, 8192), bf16),
        pltpu.VMEM((BLOCK, 1024), bf16),
        pltpu.VMEM((48, 8192), bf16),
        pltpu.VMEM((128, COLS), bf16),
        pltpu.VMEM((4, OWN, 128), bf16),
        pltpu.VMEM((BLOCK, HEAD), f32),
        pltpu.VMEM((BLOCK, HEAD), f32),
        pltpu.VMEM((16, 8192), bf16),
        pltpu.VMEM((16, 1024), bf16),
        pltpu.VMEM((4, 16, OWN), bf16),
        pltpu.VMEM((4, 16, OWN), f32),
        pltpu.VMEM((2, 16, OWN), f32),
        pltpu.VMEM((16, OWN), f32),
        pltpu.VMEM((16, OWN), bf16),
        pltpu.VMEM((32, 16, 256), f32),
        pltpu.VMEM((16, 16, 256), f32),
        pltpu.VMEM((8, 16, 256), f32),
        pltpu.VMEM((4, 16, 256), f32),
        pltpu.VMEM((2, 16, 256), f32),
        pltpu.VMEM((16, 256), f32),
        pltpu.VMEM((16, 256), f32),
        pltpu.VMEM((16, 256), f32),
        pltpu.VMEM((16, 256), f32),
        pltpu.VMEM((8, 16, 128), f32),
        pltpu.VMEM((4, 16, 128), f32),
        pltpu.VMEM((2, 16, 128), f32),
        pltpu.VMEM((16, 128), f32),
        pltpu.VMEM((16, 128), f32),
        pltpu.VMEM((16, 128), f32),
        pltpu.VMEM((16, 128), f32),
        pltpu.VMEM((32, 16, 256), f32),
        pltpu.VMEM((8, 16, 128), f32),
        pltpu.SemaphoreType.DMA((14,)),
        pltpu.SemaphoreType.DMA((41,)),
        pltpu.SemaphoreType.DMA((PIECES, 2)),
        pltpu.SemaphoreType.DMA((3, GROUPS)),
        pltpu.SemaphoreType.DMA((3, GROUPS)),
        pltpu.SemaphoreType.DMA((27,)),
        pltpu.SemaphoreType.DMA((27,)),
    ]
    queries, kv, down_t, up_t = pl.pallas_call(
        project,
        out_shape=(
            jax.ShapeDtypeStruct((BLOCK, 1024), bf16),
            jax.ShapeDtypeStruct((2, 2 * BLOCK, HEAD), bf16),
            jax.ShapeDtypeStruct((16, 1024), f32),
            jax.ShapeDtypeStruct((16, 8192), f32),
        ),
        in_specs=[hbm, vmem] + [hbm] * 13,
        out_specs=(vmem, vmem, vmem, vmem),
        scratch_shapes=scratch,
        compiler_params=pltpu.CompilerParams(
            collective_id=0, has_side_effects=True, vmem_limit_bytes=62 * 1024 * 1024
        ),
        name="project",
    )(
        states_forward, norm_gain.reshape(1, 8192), query_weight, frozen_key_weight, frozen_value_weight,
        query_down.T, key_down_matrix.T, value_down_matrix.T, query_up, key_up_matrix, value_up_matrix,
        saved_context, output_gradient, out_down.T, out_up,
    )
    station = lax.axis_index("seq")
    flag = ((station - shifted) % 2).astype(jnp.int32)
    context = pl.pallas_call(
        attend,
        grid=(HEADS,),
        out_shape=jax.ShapeDtypeStruct((BLOCK, 1024), bf16),
        in_specs=[
            pl.BlockSpec(memory_space=pltpu.SMEM),
            pl.BlockSpec((BLOCK, HEAD), lambda h: (0, h)),
            pl.BlockSpec((None, 2 * BLOCK, HEAD), lambda h: (0, 0, 0)),
            pl.BlockSpec((None, 2 * BLOCK, HEAD), lambda h: (1, 0, 0)),
        ],
        out_specs=pl.BlockSpec((BLOCK, HEAD), lambda h: (0, h)),
        compiler_params=pltpu.CompilerParams(vmem_limit_bytes=48 * 1024 * 1024),
        name="attend",
    )(flag, queries, kv, kv)
    return context, down_t.T, up_t


def solution(mesh):
    placed = (
        P(("seq", "tensor"), None),
        P(),
        P("seq", "tensor"),
        P("seq", "tensor"),
        P("seq", "tensor"),
        P(),
        P(None, "tensor"),
        P(),
        P(None, "tensor"),
        P(),
        P(None, "tensor"),
        P("tensor"),
        P("seq", "tensor"),
        P(("seq", "tensor"), None),
        P("tensor", None),
        P(),
    )
    return jax.shard_map(
        on_device,
        mesh=mesh,
        in_specs=placed,
        out_specs=(P("seq", "tensor"), P("tensor", None), P()),
        check_vma=False,
    )
```

```python
import math

import jax
import jax.numpy as jnp
from jax import lax
from jax.experimental import pallas as pl
from jax.experimental.pallas import tpu as pltpu
from jax.sharding import PartitionSpec as P

HEAD = 128
EPS = 1e-05
ADAPTER_SCALE = 2.0
ROPE_STRETCH = 0.125
BLOCK = 1024
OWN = 256
PIECE = 256
PIECES = 32
COLS = 1280
HEADS = 8
NT = (((1,), (1,)), ((), ()))
MESH = pl.DeviceIdType.MESH

ORDER = [
    (0, 0, 0),
    (0, 3, 0), (0, 1, 0), (0, 0, 3), (0, 0, 1),
    (1, 0, 0),
    (0, 2, 0), (0, 0, 2),
    (1, 3, 0), (1, 1, 0), (1, 0, 3), (1, 0, 1),
    (1, 2, 0), (1, 0, 2),
    (1, 3, 3), (1, 1, 3), (0, 3, 3), (0, 3, 1),
    (1, 2, 3), (0, 3, 2),
    (1, 3, 1), (1, 1, 1), (0, 1, 3), (0, 1, 1),
    (1, 2, 1), (0, 1, 2),
    (1, 3, 2), (1, 1, 2), (0, 2, 3), (0, 2, 1),
    (1, 2, 2), (0, 2, 2),
]
SLOT = {piece: at for at, piece in enumerate(ORDER)}
GROUPS = 16
SPAN = PIECES // GROUPS
FIRST = 4
MEET = [8, 9, 10, 12, 14, 15, 16, 19, 20, 21, 22, 24, 26, 27, 31, 31]


def f32_dot(a, b, dims=(((1,), (0,)), ((), ()))):
    return lax.dot_general(a, b, dims, preferred_element_type=jnp.float32)


def project(
    flag, states, gain, wq, wk, wv, downs_q, downs_k, downs_v, up_q, up_k, up_v, saved, grad, odown, oup,
    context, dgrad, ugrad,
    w, nb, acc, big, sc, dn_cat, up_cat, low, cos_t, sin_t, oup_v, od_v,
    lg, part, part_r1, part_r2, ctx, up, up_r3, up_r4, up_r5, up_rx, up_rz, dn, dn_r5, dn_rx, dn_rz, up_g, dn_g,
    q_v, k_own, v_own, k_prior, v_prior,
    local, w_send, w_recv, n_send, n_recv, g_send, g_recv,
):
    s = lax.axis_index("seq")
    t = lax.axis_index("tensor")
    z = s % 4
    yh = (s // 4) % 2
    x = s // 8
    yl = t // 2
    core = t % 2

    def dev(x=x, yh=yh, z=z, yl=yl, core=core):
        return ((x * 2 + yh) * 4 + z, yl * 2 + core)

    side = {
        ("x", 1): dev(x=(x + 1) % 4),
        ("x", -1): dev(x=(x + 3) % 4),
        ("z", 1): dev(z=(z + 1) % 4),
        ("z", -1): dev(z=(z + 3) % 4),
    }
    p_core = dev(core=1 - core)
    p_yl = dev(yl=1 - yl)
    p_yh = dev(yh=1 - yh)
    x_others = [dev(x=(x + d) % 4) for d in (1, 2, 3)]
    z_others = [dev(z=(z + d) % 4) for d in (1, 2, 3)]
    later = ((s + 1) % 32, t)
    before = ((s + 31) % 32, t)

    def local_copy(src, dst, at):
        return pltpu.make_async_copy(src, dst, local.at[at])

    own_w = [
        local_copy(wq, w.at[0, :, 0:1024], 0),
        local_copy(wk, w.at[0, :, 1024:1152], 1),
        local_copy(wv, w.at[0, :, 1152:1280], 2),
    ]
    for c in own_w:
        c.start()
    load_states = local_copy(states, big, 3)
    load_states.start()

    v_own[:, 128:256] = jnp.ones((BLOCK, 128), jnp.bfloat16)
    v_prior[:, 128:256] = jnp.ones((BLOCK, 128), jnp.bfloat16)

    barrier = pltpu.get_barrier_semaphore()
    greeted = x_others + z_others + [p_core, p_yl, p_yh, later, before]
    for d in greeted:
        pl.semaphore_signal(barrier, inc=1, device_id=d, device_id_type=MESH)
    pl.semaphore_wait(barrier, len(greeted))

    sends = []

    def remote(src, dst, send, recv, to):
        c = pltpu.make_async_remote_copy(
            src_ref=src, dst_ref=dst, send_sem=send, recv_sem=recv, device_id=to, device_id_type=MESH
        )
        c.start()
        sends.append(c)
        return c

    arrivals = {}
    moves = []

    def move(piece, axis, way, half=None):
        o, rx, rz = piece
        at = {"x": rx, "z": rz}
        at[axis] = (at[axis] - way) % 4
        to = SLOT[(o, at["x"], at["z"])]
        frm = SLOT[piece]
        rows = slice(0, PIECE) if half is None else slice(half * 128, half * 128 + 128)
        moves.append(to)
        c = remote(
            w.at[frm, rows], w.at[to, rows], w_send.at[len(moves)], w_recv.at[to, half or 0], side[(axis, way)]
        )
        arrivals.setdefault(to, []).append(c)

    waiting = []

    def pass_on(piece, now=True):
        o, rx, rz = piece
        first, second = ("x", "z") if o == 0 else ("z", "x")
        r1, r2 = (rx, rz) if o == 0 else (rz, rx)
        if r2 == 0:
            if r1 == 0:
                move(piece, first, 1)
                move(piece, first, -1)
            elif r1 == 3:
                move(piece, first, 1, 0)
            elif r1 == 1:
                move(piece, first, -1, 1)
            if now:
                move(piece, second, 1)
                move(piece, second, -1)
            else:
                waiting.append((piece, second))
        elif r2 == 3:
            move(piece, second, 1, 0)
        elif r2 == 1:
            move(piece, second, -1, 1)

    for c in own_w:
        c.wait()
    other = remote(w.at[0], w.at[SLOT[(1, 0, 0)]], w_send.at[0], w_recv.at[SLOT[(1, 0, 0)], 0], p_yh)
    pass_on((0, 0, 0))

    loads = [
        local_copy(downs_q, dn_cat.at[0:16], 4),
        local_copy(downs_k, dn_cat.at[16:32], 5),
        local_copy(downs_v, dn_cat.at[32:48], 6),
        local_copy(oup, oup_v, 10),
        local_copy(odown, od_v, 11),
        local_copy(saved, sc, 12),
    ]
    for c in loads:
        c.start()

    load_states.wait()

    def squares(c, total):
        at = pl.multiple_of(c * 256, 256)
        one = big[:, pl.ds(at, 128)].astype(jnp.float32)
        two = big[:, pl.ds(at + 128, 128)].astype(jnp.float32)
        return total + (one * one + two * two)

    total = lax.fori_loop(0, 32, squares, jnp.zeros((OWN, 128), jnp.float32))
    factor = lax.rsqrt(jnp.sum(total, axis=1, keepdims=True) / 8192.0 + EPS)

    def source(piece):
        o, rx, rz = piece
        return (((x + rx) % 4) * 2 + (yh + o) % 2) * 4 + (z + rz) % 4

    def columns(g):
        return pl.ds(g * SPAN, SPAN)

    def normed(g):
        for j in range(g * SPAN, (g + 1) * SPAN):
            at = pl.multiple_of(source(ORDER[j]) * PIECE, PIECE)
            wide = big[:, pl.ds(at, PIECE)].astype(jnp.float32)
            scale = gain[:, pl.ds(at, PIECE)].astype(jnp.float32)
            nb[t, j] = (wide * factor * scale).astype(jnp.bfloat16)

    n_mine = {}

    def send_normed(g):
        mine = nb.at[t, columns(g)]
        n_mine[g] = (
            remote(mine, mine, n_send.at[0, g], n_recv.at[0, g], p_yl),
            remote(mine, mine, n_send.at[1, g], n_recv.at[1, g], p_core),
        )

    for g in range(GROUPS):
        normed(g)
        if g < 2:
            send_normed(g)

    exchanges = {}

    def swap(at, src, dst, to):
        exchanges[at] = remote(src, dst, g_send.at[at], g_recv.at[at], to)

    def got(at):
        exchanges[at].wait_recv()

    load_grad = local_copy(grad, big, 13)
    load_grad.start()
    for c in loads[:3]:
        c.wait()

    total = jnp.zeros((OWN, 48), jnp.float32)
    for j in range(PIECES):
        at = pl.multiple_of(source(ORDER[j]) * PIECE, PIECE)
        total = total + f32_dot(nb[t, j], dn_cat[:, pl.ds(at, PIECE)], NT)
    low[t, :, 0:48] = total.astype(jnp.bfloat16)
    low[t, :, 48:128] = jnp.zeros((OWN, 80), jnp.bfloat16)

    up_cat[...] = jnp.zeros_like(up_cat)
    ups = [
        local_copy(up_q, up_cat.at[0:16, 0:1024], 7),
        local_copy(up_k, up_cat.at[16:32, 1024:1152], 8),
        local_copy(up_v, up_cat.at[32:48, 1152:1280], 9),
    ]
    for c in ups:
        c.start()

    lane = lax.broadcasted_iota(jnp.int32, (256, HEAD), 1)
    index = (lane % 64).astype(jnp.float32)
    inverse = jnp.exp(index * (-2.0 * math.log(10000.0) / HEAD))
    sign = jnp.where(lane < 64, -1.0, 1.0).astype(jnp.float32)

    def tables(i, carry):
        at = pl.multiple_of(i * 256, 256)
        position = lax.broadcasted_iota(jnp.int32, (256, HEAD), 0) + (s * BLOCK + at)
        angle = position.astype(jnp.float32) * ROPE_STRETCH * inverse
        cos_t[pl.ds(at, 256), :] = jnp.cos(angle)
        sin_t[pl.ds(at, 256), :] = jnp.sin(angle) * sign
        return carry

    for c in loads[3:]:
        c.wait()
    load_grad.wait()

    u3, u4, u5 = core * 16, core * 16 + yl * 8, core * 16 + yl * 8 + yh * 4
    v3, v4, v5 = (1 - core) * 16, u3 + (1 - yl) * 8, u4 + (1 - yh) * 4
    d5, e5 = yh * 4, (1 - yh) * 4
    theirs = (1 - yl) * 2 + core

    def g0():
        total = jnp.zeros((16, OWN), jnp.float32)
        for c in range(16):
            cols = slice(c * 512, c * 512 + 512)
            total = total + f32_dot(oup_v[:, cols], big[:, cols], NT)
        lg[t] = total.astype(jnp.bfloat16)
        for b in range(4):
            part[b] = f32_dot(od_v[...], sc[b * 256 : b * 256 + 256, :], NT)
        swap(0, part.at[pl.ds((1 - yl) * 2, 2)], part_r1, p_yl)
        swap(1, lg.at[t], lg.at[t], p_yl)
        swap(2, lg.at[t], lg.at[t], p_core)

    def send_low():
        swap(3, low.at[t], low.at[t], p_yl)
        swap(4, low.at[t], low.at[t], p_core)

    def g1():
        got(0)
        keep = pl.ds(yl * 2, 2)
        part[keep] = part[keep] + part_r1[...]
        swap(5, part.at[yl * 2 + 1 - core], part_r2, p_core)
        got(1)
        swap(6, lg.at[theirs], lg.at[theirs], p_core)
        got(3)
        swap(7, low.at[theirs], low.at[theirs], p_core)

    def g2():
        got(5)
        ctx[...] = (part[t] + part_r2[...]).astype(jnp.bfloat16)
        for b in range(32):
            up[b] = ADAPTER_SCALE * f32_dot(ctx[...], big[:, b * 256 : b * 256 + 256])
        swap(8, up.at[pl.ds(v3, 16)], up_r3, p_core)
        got(2)
        got(6)
        for b in range(8):
            sums = jnp.zeros((16, 128), jnp.float32)
            for k in range(4):
                sums = sums + f32_dot(lg[k], sc[k * 256 : k * 256 + 256, b * 128 : b * 128 + 128])
            dn[b] = ADAPTER_SCALE * sums

    def g3():
        got(8)
        up[pl.ds(u3, 16)] = up[pl.ds(u3, 16)] + up_r3[...]
        swap(9, up.at[pl.ds(v4, 8)], up_r4, p_yl)

    def g4():
        got(9)
        up[pl.ds(u4, 8)] = up[pl.ds(u4, 8)] + up_r4[...]
        swap(10, up.at[pl.ds(v5, 4)], up_r5, p_yh)
        swap(11, dn.at[pl.ds(e5, 4)], dn_r5, p_yh)

    def g5():
        got(10)
        got(11)
        up[pl.ds(u5, 4)] = up[pl.ds(u5, 4)] + up_r5[...]
        dn[pl.ds(d5, 4)] = dn[pl.ds(d5, 4)] + dn_r5[...]
        for k in range(3):
            there = (x + k + 1) % 4
            swap(12 + k, up.at[u5 + there], up_rx.at[k], x_others[k])
            swap(15 + k, dn.at[d5 + there], dn_rx.at[k], x_others[k])

    def g6():
        for k in range(6):
            got(12 + k)
        up_rz[z] = up[u5 + x] + up_rx[0] + up_rx[1] + up_rx[2]
        dn_rz[z] = dn[d5 + x] + dn_rx[0] + dn_rx[1] + dn_rx[2]
        for k in range(3):
            swap(18 + k, up_rz.at[z], up_rz.at[z], z_others[k])
            swap(21 + k, dn_rz.at[z], dn_rz.at[z], z_others[k])

    def g7():
        for k in range(6):
            got(18 + k)
        up_g[u5 + x] = up_rz[0] + up_rz[1] + up_rz[2] + up_rz[3]
        dn_g[d5 + x] = dn_rz[0] + dn_rz[1] + dn_rz[2] + dn_rz[3]
        for k in range(3):
            swap(24 + k, up_g.at[u5 + x], up_g.at[u5 + x], x_others[k])
            swap(27 + k, dn_g.at[d5 + x], dn_g.at[d5 + x], x_others[k])

    def g8():
        for k in range(6):
            got(24 + k)
        swap(30, up_g.at[pl.ds(u5, 4)], up_g.at[pl.ds(u5, 4)], p_yh)
        swap(31, dn_g.at[pl.ds(d5, 4)], dn_g.at[pl.ds(d5, 4)], p_yh)

    def g9():
        got(30)
        swap(32, up_g.at[pl.ds(u4, 8)], up_g.at[pl.ds(u4, 8)], p_yl)
        got(31)
        for b in range(8):
            dgrad[:, b * 128 : b * 128 + 128] = dn_g[b]

    def g10():
        got(32)
        swap(33, up_g.at[pl.ds(u3, 16)], up_g.at[pl.ds(u3, 16)], p_core)

    def g11():
        got(33)
        for b in range(32):
            ugrad[:, b * 256 : b * 256 + 256] = up_g[b]

    def adapter():
        got(4)
        got(7)
        for c in ups:
            c.wait()

        def rows_of(i, carry):
            rows = pl.ds(pl.multiple_of(i * 256, 256), 256)
            for c in range(5):
                cols = slice(c * 256, c * 256 + 256)
                acc[rows, cols] += ADAPTER_SCALE * f32_dot(low[i], up_cat[:, cols])
            return carry

        lax.fori_loop(0, 4, rows_of, 0)

    def multiply(ja, jb):
        def rows_of(i, carry):
            rows = pl.ds(pl.multiple_of(i * 256, 256), 256)
            for c in range(5):
                cols = slice(c * 256, c * 256 + 256)
                both = f32_dot(nb[i, ja], w[ja, :, cols]) + f32_dot(nb[i, jb], w[jb, :, cols])
                acc[rows, cols] = both if ja == 0 else acc[rows, cols] + both
            return carry

        lax.fori_loop(0, 4, rows_of, 0)

    passed = []

    def meet(g):
        n_mine[g][0].wait_recv()
        there = nb.at[theirs, columns(g)]
        fwd = remote(there, there, n_send.at[2, g], n_recv.at[2, g], p_core)
        passed.append((g, fwd))

    def multiply_next():
        g, fwd = passed.pop(0)
        n_mine[g][1].wait_recv()
        fwd.wait_recv()
        multiply(g * SPAN, g * SPAN + 1)

    g0()
    send_low()
    for g in range(2, FIRST):
        send_normed(g)

    hooks = {
        7: [lambda: lax.fori_loop(0, 4, tables, 0)],
        11: [g1],
        13: [g2, adapter],
        14: [g3],
        20: [g4],
        24: [g5],
        30: [g6],
    }
    arrivals[SLOT[(1, 0, 0)]] = [other]
    sent = FIRST
    for j in range(PIECES):
        if j > 0:
            for c in arrivals[j]:
                c.wait_recv()
            pass_on(ORDER[j], now=j >= 5)
            if j == 5:
                for piece, axis in waiting:
                    move(piece, axis, 1)
                    move(piece, axis, -1)
        if j % 2 == 0 and j > 0 and sent < GROUPS:
            send_normed(sent)
            sent += 1
        for f in hooks.get(j, []):
            f()
        for g in range(GROUPS):
            if MEET[g] == j:
                meet(g)
                if len(passed) > 1:
                    multiply_next()
    while passed:
        multiply_next()

    def rotated(value, rows):
        return value * cos_t[rows, :] + pltpu.roll(value, 64, 1) * sin_t[rows, :]

    def keys_of(i, carry):
        rows = pl.ds(pl.multiple_of(i * 256, 256), 256)
        k_own[rows, :] = rotated(acc[rows, 1024:1152], rows).astype(jnp.bfloat16)
        v_own[rows, 0:128] = acc[rows, 1152:1280].astype(jnp.bfloat16)
        return carry

    lax.fori_loop(0, 4, keys_of, 0)
    swap(34, k_own, k_prior, later)
    swap(35, v_own.at[:, 0:128], v_prior.at[:, 0:128], later)

    to_exponent = math.log2(math.e) / math.sqrt(HEAD)

    def queries_of(i, carry):
        rows = pl.ds(pl.multiple_of(i * 256, 256), 256)
        for h in range(HEADS):
            cols = slice(h * HEAD, h * HEAD + HEAD)
            q_v[rows, cols] = (rotated(acc[rows, cols], rows) * to_exponent).astype(jnp.bfloat16)
        return carry

    lax.fori_loop(0, 4, queries_of, 0)

    bias = jnp.where(flag[0] == 1, 0.0, -1e30).astype(jnp.float32)
    key = lax.broadcasted_iota(jnp.int32, (256, 256), 1)
    query = lax.broadcasted_iota(jnp.int32, (256, 256), 0)
    place = lax.broadcasted_iota(jnp.int32, (256, HEAD), 1)

    def own_keys(h, carry):
        cols = pl.ds(pl.multiple_of(h * HEAD, HEAD), HEAD)
        for i in range(4):
            rows = slice(i * 256, i * 256 + 256)
            queries = q_v[rows, cols]
            corner = f32_dot(queries, k_own[rows, :], NT)
            corner = jnp.where(key <= query, corner, -jnp.inf)
            summit = jnp.max(corner, axis=1, keepdims=True)
            if i > 0:
                scores = f32_dot(queries, k_own[0 : i * 256, :], NT)
                summit = jnp.maximum(summit, jnp.max(scores, axis=1, keepdims=True))
            raised = jnp.exp2(corner - summit).astype(jnp.bfloat16)
            found = f32_dot(raised, v_own[rows, :])
            if i > 0:
                raised = jnp.exp2(scores - summit).astype(jnp.bfloat16)
                found = found + f32_dot(raised, v_own[0 : i * 256, :])
            acc[rows, cols] = found[:, 0:128]
            acc[rows, 1024:1152] = jnp.where(place == h, found[:, 128:256], acc[rows, 1024:1152])
            acc[rows, 1152:1280] = jnp.where(place == h, summit, acc[rows, 1152:1280])
        return carry

    def prior_keys(h, carry):
        cols = pl.ds(pl.multiple_of(h * HEAD, HEAD), HEAD)
        for i in range(4):
            rows = slice(i * 256, i * 256 + 256)
            scores = f32_dot(q_v[rows, cols], k_prior[...], NT)
            norm = jnp.sum(jnp.where(place == h, acc[rows, 1024:1152], 0.0), axis=1, keepdims=True)
            before = jnp.max(jnp.where(place == h, acc[rows, 1152:1280], -jnp.inf), axis=1, keepdims=True)
            summit = jnp.maximum(before, jnp.max(scores, axis=1, keepdims=True) + bias)
            raised = jnp.exp2(scores - (summit - bias)).astype(jnp.bfloat16)
            found = f32_dot(raised, v_prior[...])
            shrink = jnp.exp2(before - summit)
            total = acc[rows, cols] * shrink + found[:, 0:128]
            norm = norm * shrink + found[:, 128:256]
            q_v[rows, cols] = (total / norm).astype(jnp.bfloat16)
        return carry

    lax.fori_loop(0, 4, own_keys, 0)
    g7()
    lax.fori_loop(4, 8, own_keys, 0)
    g8()
    got(34)
    got(35)
    stores = []
    for h in range(0, HEADS, 2):
        lax.fori_loop(h, h + 2, prior_keys, 0)
        cols = slice(h * HEAD, (h + 2) * HEAD)
        stores.append(pltpu.make_async_copy(q_v.at[:, cols], context.at[:, cols], local.at[14 + h // 2]))
        stores[-1].start()
        if h == 0:
            g9()
        elif h == 2:
            g10()
        elif h == 4:
            g11()
    for c in stores:
        c.wait()
    for c in sends:
        c.wait_send()


def on_device(
    states_forward, norm_gain, query_weight, frozen_key_weight, frozen_value_weight, query_down, query_up,
    key_down_matrix, key_up_matrix, value_down_matrix, value_up_matrix, shifted, saved_context, output_gradient,
    out_down, out_up,
):
    bf16, f32 = jnp.bfloat16, jnp.float32
    hbm = pl.BlockSpec(memory_space=pl.ANY)
    vmem = pl.BlockSpec(memory_space=pltpu.VMEM)
    scratch = [
        pltpu.VMEM((PIECES, PIECE, COLS), bf16),
        pltpu.VMEM((4, PIECES, OWN, PIECE), bf16),
        pltpu.VMEM((BLOCK, COLS), f32),
        pltpu.VMEM((OWN, 8192), bf16),
        pltpu.VMEM((BLOCK, 1024), bf16),
        pltpu.VMEM((48, 8192), bf16),
        pltpu.VMEM((128, COLS), bf16),
        pltpu.VMEM((4, OWN, 128), bf16),
        pltpu.VMEM((BLOCK, HEAD), f32),
        pltpu.VMEM((BLOCK, HEAD), f32),
        pltpu.VMEM((16, 8192), bf16),
        pltpu.VMEM((16, 1024), bf16),
        pltpu.VMEM((4, 16, OWN), bf16),
        pltpu.VMEM((4, 16, OWN), f32),
        pltpu.VMEM((2, 16, OWN), f32),
        pltpu.VMEM((16, OWN), f32),
        pltpu.VMEM((16, OWN), bf16),
        pltpu.VMEM((32, 16, 256), f32),
        pltpu.VMEM((16, 16, 256), f32),
        pltpu.VMEM((8, 16, 256), f32),
        pltpu.VMEM((4, 16, 256), f32),
        pltpu.VMEM((3, 16, 256), f32),
        pltpu.VMEM((4, 16, 256), f32),
        pltpu.VMEM((8, 16, 128), f32),
        pltpu.VMEM((4, 16, 128), f32),
        pltpu.VMEM((3, 16, 128), f32),
        pltpu.VMEM((4, 16, 128), f32),
        pltpu.VMEM((32, 16, 256), f32),
        pltpu.VMEM((8, 16, 128), f32),
        pltpu.VMEM((BLOCK, 1024), bf16),
        pltpu.VMEM((BLOCK, HEAD), bf16),
        pltpu.VMEM((BLOCK, 2 * HEAD), bf16),
        pltpu.VMEM((BLOCK, HEAD), bf16),
        pltpu.VMEM((BLOCK, 2 * HEAD), bf16),
        pltpu.SemaphoreType.DMA((18,)),
        pltpu.SemaphoreType.DMA((41,)),
        pltpu.SemaphoreType.DMA((PIECES, 2)),
        pltpu.SemaphoreType.DMA((3, GROUPS)),
        pltpu.SemaphoreType.DMA((3, GROUPS)),
        pltpu.SemaphoreType.DMA((36,)),
        pltpu.SemaphoreType.DMA((36,)),
    ]
    station = lax.axis_index("seq")
    flag = ((station - shifted) % 2).astype(jnp.int32)
    context, down_t, up_t = pl.pallas_call(
        project,
        out_shape=(
            jax.ShapeDtypeStruct((BLOCK, 1024), bf16),
            jax.ShapeDtypeStruct((16, 1024), f32),
            jax.ShapeDtypeStruct((16, 8192), f32),
        ),
        in_specs=[pl.BlockSpec(memory_space=pltpu.SMEM), hbm, vmem] + [hbm] * 13,
        out_specs=(hbm, vmem, vmem),
        scratch_shapes=scratch,
        compiler_params=pltpu.CompilerParams(
            collective_id=0, has_side_effects=True, vmem_limit_bytes=64 * 1024 * 1024
        ),
        name="fused",
    )(
        flag, states_forward, norm_gain.reshape(1, 8192), query_weight, frozen_key_weight, frozen_value_weight,
        query_down.T, key_down_matrix.T, value_down_matrix.T, query_up, key_up_matrix, value_up_matrix,
        saved_context, output_gradient, out_down.T, out_up,
    )
    return context, down_t.T, up_t


def solution(mesh):
    placed = (
        P(("seq", "tensor"), None),
        P(),
        P("seq", "tensor"),
        P("seq", "tensor"),
        P("seq", "tensor"),
        P(),
        P(None, "tensor"),
        P(),
        P(None, "tensor"),
        P(),
        P(None, "tensor"),
        P("tensor"),
        P("seq", "tensor"),
        P(("seq", "tensor"), None),
        P("tensor", None),
        P(),
    )
    return jax.shard_map(
        on_device,
        mesh=mesh,
        in_specs=placed,
        out_specs=(P("seq", "tensor"), P("tensor", None), P()),
        check_vma=False,
    )
```

```python
import math

import jax
import jax.numpy as jnp
from jax import lax
from jax.experimental import pallas as pl
from jax.experimental.pallas import tpu as pltpu
from jax.sharding import PartitionSpec as P

HEAD = 128
EPS = 1e-05
ADAPTER_SCALE = 2.0
ROPE_STRETCH = 0.125
BLOCK = 1024
OWN = 256
PIECE = 256
PIECES = 32
COLS = 1280
HEADS = 8
NT = (((1,), (1,)), ((), ()))
MESH = pl.DeviceIdType.MESH

ORDER = [
    (0, 0, 0), (0, 1, 0), (0, 3, 0), (1, 0, 0), (0, 2, 0), (0, 0, 3),
    (1, 0, 3), (0, 1, 1), (1, 1, 0), (1, 0, 1), (0, 0, 1), (0, 1, 3),
    (1, 3, 3), (1, 0, 2), (1, 3, 1), (0, 2, 1), (1, 3, 0), (0, 1, 2),
    (1, 1, 3), (1, 1, 1), (1, 1, 2), (1, 3, 2), (0, 3, 1), (0, 2, 3),
    (0, 3, 3), (1, 2, 3), (1, 2, 0), (0, 0, 2), (0, 2, 2), (1, 2, 2),
    (1, 2, 1), (0, 3, 2),
]
SLOT = {piece: at for at, piece in enumerate(ORDER)}
ORDER_RANK = {piece: piece[0] * 16 + piece[1] * 4 + piece[2] for piece in ORDER}
GROUPS = 16
SPAN = PIECES // GROUPS
FIRST = 4
MEET = [7, 8, 11, 13, 13, 14, 15, 16, 17, 23, 24, 25, 28, 28, 29, 31]
HOLD = {
    ((0, 1, 0), 'z', 1): 4,
    ((0, 3, 0), 'z', 1): 11,
    ((0, 3, 0), 'z', -1): 11,
    ((0, 1, 1), 'z', -1): 5,
    ((1, 0, 2), 'x', -1): 1,
    ((1, 1, 0), 'x', -1): 1,
    ((0, 0, 3), 'z', 1): 1,
    ((0, 1, 3), 'z', 1): 2,
    ((0, 3, 3), 'z', 1): 3,
    ((1, 0, 1), 'x', -1): 3,
    ((1, 0, 1), 'z', -1): 2,
    ((1, 0, 3), 'z', 1): 1,
    ((0, 2, 0), 'z', 1): 8,
    ((1, 0, 3), 'x', -1): 1,
    ((1, 1, 3), 'x', -1): 1,
    ((1, 1, 2), 'x', -1): 2,
    ((1, 3, 0), 'x', 1): 3,
    ((0, 2, 1), 'z', -1): 7,
    ((1, 1, 1), 'x', -1): 5,
    ((1, 3, 1), 'x', 1): 9,
    ((0, 0, 1), 'z', -1): 6,
}


def f32_dot(a, b, dims=(((1,), (0,)), ((), ()))):
    return lax.dot_general(a, b, dims, preferred_element_type=jnp.float32)


def project(
    flag, states, gain, wq, wk, wv, downs_q, downs_k, downs_v, up_q, up_k, up_v, saved, grad, odown, oup,
    context, dgrad, ugrad,
    w, nb, acc, big, sc, dn_cat, up_cat, low, cos_t, sin_t, oup_v, od_v,
    lg, part, part_r1, part_r2, ctx, up, up_r3, up_r4, up_r5, up_rx, up_rz, dn, dn_r5, dn_rx, dn_rz, up_g, dn_g,
    q_v, k_own, v_own, k_prior, v_prior,
    local, w_send, w_recv, n_send, n_recv, g_send, g_recv,
):
    s = lax.axis_index("seq")
    t = lax.axis_index("tensor")
    z = s % 4
    yh = (s // 4) % 2
    x = s // 8
    yl = t // 2
    core = t % 2

    def dev(x=x, yh=yh, z=z, yl=yl, core=core):
        return ((x * 2 + yh) * 4 + z, yl * 2 + core)

    side = {
        ("x", 1): dev(x=(x + 1) % 4),
        ("x", -1): dev(x=(x + 3) % 4),
        ("z", 1): dev(z=(z + 1) % 4),
        ("z", -1): dev(z=(z + 3) % 4),
    }
    p_core = dev(core=1 - core)
    p_yl = dev(yl=1 - yl)
    p_yh = dev(yh=1 - yh)
    x_others = [dev(x=(x + d) % 4) for d in (1, 2, 3)]
    z_others = [dev(z=(z + d) % 4) for d in (1, 2, 3)]
    later = ((s + 1) % 32, t)
    before = ((s + 31) % 32, t)

    def local_copy(src, dst, at):
        return pltpu.make_async_copy(src, dst, local.at[at])

    own_w = [
        local_copy(wq, w.at[0, :, 0:1024], 0),
        local_copy(wk, w.at[0, :, 1024:1152], 1),
        local_copy(wv, w.at[0, :, 1152:1280], 2),
    ]
    for c in own_w:
        c.start()
    load_states = local_copy(states, big, 3)
    load_states.start()

    v_own[:, 128:256] = jnp.ones((BLOCK, 128), jnp.bfloat16)
    v_prior[:, 128:256] = jnp.ones((BLOCK, 128), jnp.bfloat16)

    barrier = pltpu.get_barrier_semaphore()
    greeted = x_others + z_others + [p_core, p_yl, p_yh, later, before]
    for d in greeted:
        pl.semaphore_signal(barrier, inc=1, device_id=d, device_id_type=MESH)
    pl.semaphore_wait(barrier, len(greeted))

    sends = []

    def remote(src, dst, send, recv, to):
        c = pltpu.make_async_remote_copy(
            src_ref=src, dst_ref=dst, send_sem=send, recv_sem=recv, device_id=to, device_id_type=MESH
        )
        c.start()
        sends.append(c)
        return c

    arrivals = {}
    moves = []

    def move(piece, axis, way, half=None):
        o, rx, rz = piece
        at = {"x": rx, "z": rz}
        at[axis] = (at[axis] - way) % 4
        to = SLOT[(o, at["x"], at["z"])]
        frm = SLOT[piece]
        rows = slice(0, PIECE) if half is None else slice(half * 128, half * 128 + 128)
        moves.append(to)
        c = remote(
            w.at[frm, rows], w.at[to, rows], w_send.at[len(moves)], w_recv.at[to, half or 0], side[(axis, way)]
        )
        arrivals.setdefault(to, []).append(c)

    steps = [[] for _ in range(PIECES)]
    for at, piece in enumerate(ORDER):
        o, rx, rz = piece
        first, second = ("x", "z") if o == 0 else ("z", "x")
        r1, r2 = (rx, rz) if o == 0 else (rz, rx)
        out = []
        if r2 == 0:
            if r1 == 0:
                out += [(2, first, 1, None), (2, first, -1, None)]
            elif r1 == 3:
                out += [(0, first, 1, 0)]
            elif r1 == 1:
                out += [(0, first, -1, 1)]
            out += [(3, second, 1, None), (3, second, -1, None)]
        elif r2 == 3:
            out += [(1, second, 1, 0)]
        elif r2 == 1:
            out += [(1, second, -1, 1)]
        for rank, axis, way, half in out:
            step = min(at + HOLD.get((piece, axis, way), 0), PIECES - 1)
            steps[step].append((rank, ORDER_RANK[piece], piece, axis, way, half))

    def pass_on(j):
        for _, _, piece, axis, way, half in sorted(steps[j], key=lambda e: e[:2]):
            move(piece, axis, way, half)

    for c in own_w:
        c.wait()
    other = remote(w.at[0], w.at[SLOT[(1, 0, 0)]], w_send.at[0], w_recv.at[SLOT[(1, 0, 0)], 0], p_yh)
    pass_on(0)

    loads = [
        local_copy(downs_q, dn_cat.at[0:16], 4),
        local_copy(downs_k, dn_cat.at[16:32], 5),
        local_copy(downs_v, dn_cat.at[32:48], 6),
        local_copy(oup, oup_v, 10),
        local_copy(odown, od_v, 11),
        local_copy(saved, sc, 12),
    ]
    for c in loads:
        c.start()

    load_states.wait()

    def squares(c, total):
        at = pl.multiple_of(c * 256, 256)
        one = big[:, pl.ds(at, 128)].astype(jnp.float32)
        two = big[:, pl.ds(at + 128, 128)].astype(jnp.float32)
        return total + (one * one + two * two)

    total = lax.fori_loop(0, 32, squares, jnp.zeros((OWN, 128), jnp.float32))
    factor = lax.rsqrt(jnp.sum(total, axis=1, keepdims=True) / 8192.0 + EPS)

    def source(piece):
        o, rx, rz = piece
        return (((x + rx) % 4) * 2 + (yh + o) % 2) * 4 + (z + rz) % 4

    def columns(g):
        return pl.ds(g * SPAN, SPAN)

    def normed(g):
        for j in range(g * SPAN, (g + 1) * SPAN):
            at = pl.multiple_of(source(ORDER[j]) * PIECE, PIECE)
            wide = big[:, pl.ds(at, PIECE)].astype(jnp.float32)
            scale = gain[pl.ds(at, PIECE)].astype(jnp.float32).reshape(1, PIECE)
            nb[t, j] = (wide * factor * scale).astype(jnp.bfloat16)

    n_mine = {}

    def send_normed(g):
        mine = nb.at[t, columns(g)]
        n_mine[g] = (
            remote(mine, mine, n_send.at[0, g], n_recv.at[0, g], p_yl),
            remote(mine, mine, n_send.at[1, g], n_recv.at[1, g], p_core),
        )

    for g in range(GROUPS):
        normed(g)
        if g < 2:
            send_normed(g)

    exchanges = {}

    def swap(at, src, dst, to):
        exchanges[at] = remote(src, dst, g_send.at[at], g_recv.at[at], to)

    def got(at):
        exchanges[at].wait_recv()

    load_grad = local_copy(grad, big, 13)
    load_grad.start()
    for c in loads[:3]:
        c.wait()

    total = jnp.zeros((OWN, 48), jnp.float32)
    for j in range(PIECES):
        at = pl.multiple_of(source(ORDER[j]) * PIECE, PIECE)
        total = total + f32_dot(nb[t, j], dn_cat[:, pl.ds(at, PIECE)], NT)
    low[t, :, 0:48] = total.astype(jnp.bfloat16)
    low[t, :, 48:128] = jnp.zeros((OWN, 80), jnp.bfloat16)

    up_cat[...] = jnp.zeros_like(up_cat)
    ups = [
        local_copy(up_q, up_cat.at[0:16, 0:1024], 7),
        local_copy(up_k, up_cat.at[16:32, 1024:1152], 8),
        local_copy(up_v, up_cat.at[32:48, 1152:1280], 9),
    ]
    for c in ups:
        c.start()

    lane = lax.broadcasted_iota(jnp.int32, (256, HEAD), 1)
    index = (lane % 64).astype(jnp.float32)
    inverse = jnp.exp(index * (-2.0 * math.log(10000.0) / HEAD))
    sign = jnp.where(lane < 64, -1.0, 1.0).astype(jnp.float32)

    def tables(i, carry):
        at = pl.multiple_of(i * 256, 256)
        position = lax.broadcasted_iota(jnp.int32, (256, HEAD), 0) + (s * BLOCK + at)
        angle = position.astype(jnp.float32) * ROPE_STRETCH * inverse
        cos_t[pl.ds(at, 256), :] = jnp.cos(angle)
        sin_t[pl.ds(at, 256), :] = jnp.sin(angle) * sign
        return carry

    for c in loads[3:]:
        c.wait()
    load_grad.wait()

    u3, u4, u5 = core * 16, core * 16 + yl * 8, core * 16 + yl * 8 + yh * 4
    v3, v4, v5 = (1 - core) * 16, u3 + (1 - yl) * 8, u4 + (1 - yh) * 4
    d5, e5 = yh * 4, (1 - yh) * 4
    theirs = (1 - yl) * 2 + core

    def g0():
        total = jnp.zeros((16, OWN), jnp.float32)
        for c in range(16):
            cols = slice(c * 512, c * 512 + 512)
            total = total + f32_dot(oup_v[:, cols], big[:, cols], NT)
        lg[t] = total.astype(jnp.bfloat16)
        for b in range(4):
            part[b] = f32_dot(od_v[...], sc[b * 256 : b * 256 + 256, :], NT)
        swap(0, part.at[pl.ds((1 - yl) * 2, 2)], part_r1, p_yl)
        swap(1, lg.at[t], lg.at[t], p_yl)
        swap(2, lg.at[t], lg.at[t], p_core)

    def send_low():
        swap(3, low.at[t], low.at[t], p_yl)
        swap(4, low.at[t], low.at[t], p_core)

    def g1():
        got(0)
        keep = pl.ds(yl * 2, 2)
        part[keep] = part[keep] + part_r1[...]
        swap(5, part.at[yl * 2 + 1 - core], part_r2, p_core)
        got(1)
        swap(6, lg.at[theirs], lg.at[theirs], p_core)
        got(3)
        swap(7, low.at[theirs], low.at[theirs], p_core)

    def g2():
        got(5)
        ctx[...] = (part[t] + part_r2[...]).astype(jnp.bfloat16)
        for b in range(32):
            up[b] = ADAPTER_SCALE * f32_dot(ctx[...], big[:, b * 256 : b * 256 + 256])
        swap(8, up.at[pl.ds(v3, 16)], up_r3, p_core)
        got(2)
        got(6)
        for b in range(8):
            sums = jnp.zeros((16, 128), jnp.float32)
            for k in range(4):
                sums = sums + f32_dot(lg[k], sc[k * 256 : k * 256 + 256, b * 128 : b * 128 + 128])
            dn[b] = ADAPTER_SCALE * sums

    def g3():
        got(8)
        up[pl.ds(u3, 16)] = up[pl.ds(u3, 16)] + up_r3[...]
        swap(9, up.at[pl.ds(v4, 8)], up_r4, p_yl)

    def g4():
        got(9)
        up[pl.ds(u4, 8)] = up[pl.ds(u4, 8)] + up_r4[...]
        swap(10, up.at[pl.ds(v5, 4)], up_r5, p_yh)
        swap(11, dn.at[pl.ds(e5, 4)], dn_r5, p_yh)

    def g5():
        got(10)
        got(11)
        up[pl.ds(u5, 4)] = up[pl.ds(u5, 4)] + up_r5[...]
        dn[pl.ds(d5, 4)] = dn[pl.ds(d5, 4)] + dn_r5[...]
        for k in range(3):
            there = (x + k + 1) % 4
            swap(12 + k, up.at[u5 + there], up_rx.at[k], x_others[k])
            swap(15 + k, dn.at[d5 + there], dn_rx.at[k], x_others[k])

    def g6():
        for k in range(6):
            got(12 + k)
        up_rz[z] = up[u5 + x] + up_rx[0] + up_rx[1] + up_rx[2]
        dn_rz[z] = dn[d5 + x] + dn_rx[0] + dn_rx[1] + dn_rx[2]
        for k in range(3):
            swap(18 + k, up_rz.at[z], up_rz.at[z], z_others[k])
            swap(21 + k, dn_rz.at[z], dn_rz.at[z], z_others[k])

    def g7():
        for k in range(6):
            got(18 + k)
        up_g[u5 + x] = up_rz[0] + up_rz[1] + up_rz[2] + up_rz[3]
        dn_g[d5 + x] = dn_rz[0] + dn_rz[1] + dn_rz[2] + dn_rz[3]
        for k in range(3):
            swap(24 + k, up_g.at[u5 + x], up_g.at[u5 + x], x_others[k])
            swap(27 + k, dn_g.at[d5 + x], dn_g.at[d5 + x], x_others[k])

    def g8():
        for k in range(6):
            got(24 + k)
        swap(30, up_g.at[pl.ds(u5, 4)], up_g.at[pl.ds(u5, 4)], p_yh)
        swap(31, dn_g.at[pl.ds(d5, 4)], dn_g.at[pl.ds(d5, 4)], p_yh)

    def g9():
        got(30)
        swap(32, up_g.at[pl.ds(u4, 8)], up_g.at[pl.ds(u4, 8)], p_yl)
        got(31)
        for b in range(8):
            dgrad[:, b * 128 : b * 128 + 128] = dn_g[b]

    def g10():
        got(32)
        swap(33, up_g.at[pl.ds(u3, 16)], up_g.at[pl.ds(u3, 16)], p_core)

    def g11():
        got(33)
        for b in range(32):
            ugrad[:, b * 256 : b * 256 + 256] = up_g[b]

    def adapter():
        got(4)
        got(7)
        for c in ups:
            c.wait()

        def rows_of(i, carry):
            rows = pl.ds(pl.multiple_of(i * 256, 256), 256)
            for c in range(5):
                cols = slice(c * 256, c * 256 + 256)
                acc[rows, cols] = ADAPTER_SCALE * f32_dot(low[i], up_cat[:, cols])
            return carry

        lax.fori_loop(0, 4, rows_of, 0)

    def multiply(ja, jb):
        def rows_of(i, carry):
            rows = pl.ds(pl.multiple_of(i * 256, 256), 256)
            for c in range(5):
                cols = slice(c * 256, c * 256 + 256)
                both = f32_dot(nb[i, ja], w[ja, :, cols]) + f32_dot(nb[i, jb], w[jb, :, cols])
                acc[rows, cols] += both
            return carry

        lax.fori_loop(0, 4, rows_of, 0)

    passed = []

    def meet(g):
        n_mine[g][0].wait_recv()
        there = nb.at[theirs, columns(g)]
        fwd = remote(there, there, n_send.at[2, g], n_recv.at[2, g], p_core)
        passed.append((g, fwd))

    def multiply_next():
        g, fwd = passed.pop(0)
        n_mine[g][1].wait_recv()
        fwd.wait_recv()
        multiply(g * SPAN, g * SPAN + 1)

    g0()
    send_low()
    for g in range(2, FIRST):
        send_normed(g)

    hooks = {
        3: [lambda: lax.fori_loop(0, 4, tables, 0)],
        6: [g1],
        8: [g2, adapter],
        9: [g3],
        15: [g4],
        25: [g5],
    }
    arrivals[SLOT[(1, 0, 0)]] = [other]
    sent = FIRST
    for j in range(PIECES):
        if j > 0:
            for c in arrivals[j]:
                c.wait_recv()
            pass_on(j)
        if j % 2 == 0 and j > 0 and sent < GROUPS:
            send_normed(sent)
            sent += 1
        for f in hooks.get(j, []):
            f()
        for g in range(GROUPS):
            if MEET[g] == j:
                meet(g)
                if len(passed) > 1:
                    multiply_next()
    g6()
    while passed:
        multiply_next()

    def rotated(value, rows):
        return value * cos_t[rows, :] + pltpu.roll(value, 64, 1) * sin_t[rows, :]

    def keys_of(i, carry):
        rows = pl.ds(pl.multiple_of(i * 256, 256), 256)
        k_own[rows, :] = rotated(acc[rows, 1024:1152], rows).astype(jnp.bfloat16)
        v_own[rows, 0:128] = acc[rows, 1152:1280].astype(jnp.bfloat16)
        return carry

    lax.fori_loop(0, 4, keys_of, 0)
    swap(34, k_own, k_prior, later)
    swap(35, v_own.at[:, 0:128], v_prior.at[:, 0:128], later)

    to_exponent = math.log2(math.e) / math.sqrt(HEAD)

    def queries_of(i, carry):
        rows = pl.ds(pl.multiple_of(i * 256, 256), 256)
        for h in range(HEADS):
            cols = slice(h * HEAD, h * HEAD + HEAD)
            q_v[rows, cols] = (rotated(acc[rows, cols], rows) * to_exponent).astype(jnp.bfloat16)
        return carry

    lax.fori_loop(0, 4, queries_of, 0)

    bias = jnp.where(flag[0] == 1, 0.0, -1e30).astype(jnp.float32)
    key = lax.broadcasted_iota(jnp.int32, (256, 256), 1)
    query = lax.broadcasted_iota(jnp.int32, (256, 256), 0)
    place = lax.broadcasted_iota(jnp.int32, (256, HEAD), 1)

    def own_keys(h, carry):
        cols = pl.ds(pl.multiple_of(h * HEAD, HEAD), HEAD)

        def scores_of(i):
            return f32_dot(q_v[i * 256 : i * 256 + 256, cols], k_own[0 : i * 256 + 256, :], NT)

        later_scores = scores_of(3)
        for i in (3, 2, 1, 0):
            rows = slice(i * 256, i * 256 + 256)
            scores = later_scores
            if i > 0:
                later_scores = scores_of(i - 1)
            corner = jnp.where(key <= query, scores[:, i * 256 :], -jnp.inf)
            scores = jnp.concatenate([scores[:, : i * 256], corner], axis=1) if i > 0 else corner
            summit = jnp.max(scores, axis=1, keepdims=True)
            raised = jnp.exp2(scores - summit).astype(jnp.bfloat16)
            found = f32_dot(raised, v_own[0 : i * 256 + 256, :])
            acc[rows, cols] = found[:, 0:128]
            acc[rows, 1024:1152] = jnp.where(place == h, found[:, 128:256], acc[rows, 1024:1152])
            acc[rows, 1152:1280] = jnp.where(place == h, summit, acc[rows, 1152:1280])
        return carry

    def prior_keys(h, carry):
        cols = pl.ds(pl.multiple_of(h * HEAD, HEAD), HEAD)

        def scores_of(i):
            return f32_dot(q_v[i * 256 : i * 256 + 256, cols], k_prior[...], NT)

        later_scores = scores_of(0)
        for i in range(4):
            rows = slice(i * 256, i * 256 + 256)
            scores = later_scores
            if i < 3:
                later_scores = scores_of(i + 1)
            norm = jnp.sum(jnp.where(place == h, acc[rows, 1024:1152], 0.0), axis=1, keepdims=True)
            before = jnp.max(jnp.where(place == h, acc[rows, 1152:1280], -jnp.inf), axis=1, keepdims=True)
            summit = jnp.maximum(before, jnp.max(scores, axis=1, keepdims=True) + bias)
            raised = jnp.exp2(scores - (summit - bias)).astype(jnp.bfloat16)
            found = f32_dot(raised, v_prior[...])
            shrink = jnp.exp2(before - summit)
            total = acc[rows, cols] * shrink + found[:, 0:128]
            norm = norm * shrink + found[:, 128:256]
            sc[rows, cols] = (total / norm).astype(jnp.bfloat16)
        return carry

    lax.fori_loop(0, 4, own_keys, 0)
    g7()
    lax.fori_loop(4, 8, own_keys, 0)
    g8()
    got(34)
    got(35)
    stores = []
    for h in range(0, HEADS, 2):
        lax.fori_loop(h, h + 2, prior_keys, 0)
        cols = slice(h * HEAD, (h + 2) * HEAD)
        stores.append(pltpu.make_async_copy(sc.at[:, cols], context.at[:, cols], local.at[14 + h // 2]))
        stores[-1].start()
        if h == 0:
            g9()
        elif h == 2:
            g10()
        elif h == 4:
            g11()
    for c in stores:
        c.wait()
    for c in sends:
        c.wait_send()


def on_device(
    states_forward, norm_gain, query_weight, frozen_key_weight, frozen_value_weight, query_down, query_up,
    key_down_matrix, key_up_matrix, value_down_matrix, value_up_matrix, shifted, saved_context, output_gradient,
    out_down, out_up,
):
    bf16, f32 = jnp.bfloat16, jnp.float32
    hbm = pl.BlockSpec(memory_space=pl.ANY)
    vmem = pl.BlockSpec(memory_space=pltpu.VMEM)
    scratch = [
        pltpu.VMEM((PIECES, PIECE, COLS), bf16),
        pltpu.VMEM((4, PIECES, OWN, PIECE), bf16),
        pltpu.VMEM((BLOCK, COLS), f32),
        pltpu.VMEM((OWN, 8192), bf16),
        pltpu.VMEM((BLOCK, 1024), bf16),
        pltpu.VMEM((48, 8192), bf16),
        pltpu.VMEM((128, COLS), bf16),
        pltpu.VMEM((4, OWN, 128), bf16),
        pltpu.VMEM((BLOCK, HEAD), f32),
        pltpu.VMEM((BLOCK, HEAD), f32),
        pltpu.VMEM((16, 8192), bf16),
        pltpu.VMEM((16, 1024), bf16),
        pltpu.VMEM((4, 16, OWN), bf16),
        pltpu.VMEM((4, 16, OWN), f32),
        pltpu.VMEM((2, 16, OWN), f32),
        pltpu.VMEM((16, OWN), f32),
        pltpu.VMEM((16, OWN), bf16),
        pltpu.VMEM((32, 16, 256), f32),
        pltpu.VMEM((16, 16, 256), f32),
        pltpu.VMEM((8, 16, 256), f32),
        pltpu.VMEM((4, 16, 256), f32),
        pltpu.VMEM((3, 16, 256), f32),
        pltpu.VMEM((4, 16, 256), f32),
        pltpu.VMEM((8, 16, 128), f32),
        pltpu.VMEM((4, 16, 128), f32),
        pltpu.VMEM((3, 16, 128), f32),
        pltpu.VMEM((4, 16, 128), f32),
        pltpu.VMEM((32, 16, 256), f32),
        pltpu.VMEM((8, 16, 128), f32),
        pltpu.VMEM((BLOCK, 1024), bf16),
        pltpu.VMEM((BLOCK, HEAD), bf16),
        pltpu.VMEM((BLOCK, 2 * HEAD), bf16),
        pltpu.VMEM((BLOCK, HEAD), bf16),
        pltpu.VMEM((BLOCK, 2 * HEAD), bf16),
        pltpu.SemaphoreType.DMA((18,)),
        pltpu.SemaphoreType.DMA((41,)),
        pltpu.SemaphoreType.DMA((PIECES, 2)),
        pltpu.SemaphoreType.DMA((3, GROUPS)),
        pltpu.SemaphoreType.DMA((3, GROUPS)),
        pltpu.SemaphoreType.DMA((36,)),
        pltpu.SemaphoreType.DMA((36,)),
    ]
    station = lax.axis_index("seq")
    flag = ((station - shifted) % 2).astype(jnp.int32)
    context, down_t, up_t = pl.pallas_call(
        project,
        out_shape=(
            jax.ShapeDtypeStruct((BLOCK, 1024), bf16),
            jax.ShapeDtypeStruct((16, 1024), f32),
            jax.ShapeDtypeStruct((16, 8192), f32),
        ),
        in_specs=[pl.BlockSpec(memory_space=pltpu.SMEM), hbm, vmem] + [hbm] * 13,
        out_specs=(hbm, vmem, vmem),
        scratch_shapes=scratch,
        compiler_params=pltpu.CompilerParams(
            collective_id=0, has_side_effects=True, vmem_limit_bytes=64 * 1024 * 1024
        ),
        name="fused",
    )(
        flag, states_forward, norm_gain, query_weight, frozen_key_weight, frozen_value_weight,
        query_down.T, key_down_matrix.T, value_down_matrix.T, query_up, key_up_matrix, value_up_matrix,
        saved_context, output_gradient, out_down.T, out_up,
    )
    return context, down_t.T, up_t


def solution(mesh):
    placed = (
        P(("seq", "tensor"), None),
        P(),
        P("seq", "tensor"),
        P("seq", "tensor"),
        P("seq", "tensor"),
        P(),
        P(None, "tensor"),
        P(),
        P(None, "tensor"),
        P(),
        P(None, "tensor"),
        P("tensor"),
        P("seq", "tensor"),
        P(("seq", "tensor"), None),
        P("tensor", None),
        P(),
    )
    return jax.shard_map(
        on_device,
        mesh=mesh,
        in_specs=placed,
        out_specs=(P("seq", "tensor"), P("tensor", None), P()),
        check_vma=False,
    )
```

```python
import math

import jax
import jax.numpy as jnp
from jax import lax
from jax.experimental import pallas as pl
from jax.experimental.pallas import tpu as pltpu
from jax.sharding import PartitionSpec as P

HEAD = 128
EPS = 1e-05
ADAPTER_SCALE = 2.0
ROPE_STRETCH = 0.125
BLOCK = 1024
OWN = 256
PIECE = 256
PIECES = 32
COLS = 1280
HEADS = 8
NT = (((1,), (1,)), ((), ()))
MESH = pl.DeviceIdType.MESH

ORDER = [
    (0, 0, 0), (0, 1, 0), (0, 3, 0), (1, 0, 0), (0, 2, 0), (0, 0, 3),
    (1, 0, 3), (0, 1, 1), (1, 1, 0), (1, 0, 1), (0, 0, 1), (0, 1, 3),
    (1, 3, 3), (1, 0, 2), (1, 3, 1), (0, 2, 1), (1, 3, 0), (0, 1, 2),
    (1, 1, 3), (1, 1, 1), (1, 1, 2), (1, 3, 2), (0, 3, 1), (0, 2, 3),
    (0, 3, 3), (1, 2, 3), (1, 2, 0), (0, 0, 2), (0, 2, 2), (1, 2, 2),
    (1, 2, 1), (0, 3, 2),
]
SLOT = {piece: at for at, piece in enumerate(ORDER)}
ORDER_RANK = {piece: piece[0] * 16 + piece[1] * 4 + piece[2] for piece in ORDER}
GROUPS = 16
SPAN = PIECES // GROUPS
FIRST = 4
MEET = [7, 8, 11, 13, 13, 14, 15, 16, 17, 23, 24, 25, 28, 28, 29, 31]
HOLD = {
    ((0, 1, 0), 'z', 1): 4,
    ((0, 3, 0), 'z', 1): 11,
    ((0, 3, 0), 'z', -1): 11,
    ((0, 1, 1), 'z', -1): 5,
    ((1, 0, 2), 'x', -1): 1,
    ((1, 1, 0), 'x', -1): 1,
    ((0, 0, 3), 'z', 1): 1,
    ((0, 1, 3), 'z', 1): 2,
    ((0, 3, 3), 'z', 1): 3,
    ((1, 0, 1), 'x', -1): 3,
    ((1, 0, 1), 'z', -1): 2,
    ((1, 0, 3), 'z', 1): 1,
    ((0, 2, 0), 'z', 1): 8,
    ((1, 0, 3), 'x', -1): 1,
    ((1, 1, 3), 'x', -1): 1,
    ((1, 1, 2), 'x', -1): 2,
    ((1, 3, 0), 'x', 1): 3,
    ((0, 2, 1), 'z', -1): 7,
    ((1, 1, 1), 'x', -1): 5,
    ((1, 3, 1), 'x', 1): 9,
    ((0, 0, 1), 'z', -1): 6,
}


def f32_dot(a, b, dims=(((1,), (0,)), ((), ()))):
    return lax.dot_general(a, b, dims, preferred_element_type=jnp.float32)


def project(
    flag, states, gain, wq, wk, wv, downs_q, downs_k, downs_v, up_q, up_k, up_v, saved, grad, odown, oup,
    context, dgrad, ugrad,
    w, nb, acc, big, sc, dn_cat, up_cat, low, cos_t, sin_t, oup_v, od_v,
    lg, part, part_r1, part_r2, ctx, up, up_r3, up_r4, up_r5, up_rx, up_rz, dn, dn_r5, dn_rx, dn_rz, up_g, dn_g,
    q_v, k_own, v_own, k_prior, v_prior,
    local, w_send, w_recv, n_send, n_recv, g_send, g_recv,
):
    s = lax.axis_index("seq")
    t = lax.axis_index("tensor")
    z = s % 4
    yh = (s // 4) % 2
    x = s // 8
    yl = t // 2
    core = t % 2

    def dev(x=x, yh=yh, z=z, yl=yl, core=core):
        return ((x * 2 + yh) * 4 + z, yl * 2 + core)

    side = {
        ("x", 1): dev(x=(x + 1) % 4),
        ("x", -1): dev(x=(x + 3) % 4),
        ("z", 1): dev(z=(z + 1) % 4),
        ("z", -1): dev(z=(z + 3) % 4),
    }
    p_core = dev(core=1 - core)
    p_yl = dev(yl=1 - yl)
    p_yh = dev(yh=1 - yh)
    x_others = [dev(x=(x + d) % 4) for d in (1, 2, 3)]
    z_others = [dev(z=(z + d) % 4) for d in (1, 2, 3)]
    later = ((s + 1) % 32, t)
    before = ((s + 31) % 32, t)

    def local_copy(src, dst, at):
        return pltpu.make_async_copy(src, dst, local.at[at])

    own_w = [
        local_copy(wq, w.at[0, :, 0:1024], 0),
        local_copy(wk, w.at[0, :, 1024:1152], 1),
        local_copy(wv, w.at[0, :, 1152:1280], 2),
    ]
    for c in own_w:
        c.start()
    load_states = local_copy(states, big, 3)
    load_states.start()

    v_own[:, 128:256] = jnp.ones((BLOCK, 128), jnp.bfloat16)
    v_prior[:, 128:256] = jnp.ones((BLOCK, 128), jnp.bfloat16)

    barrier = pltpu.get_barrier_semaphore()
    greeted = x_others + z_others + [p_core, p_yl, p_yh, later, before]
    for d in greeted:
        pl.semaphore_signal(barrier, inc=1, device_id=d, device_id_type=MESH)
    pl.semaphore_wait(barrier, len(greeted))

    sends = []

    def remote(src, dst, send, recv, to):
        c = pltpu.make_async_remote_copy(
            src_ref=src, dst_ref=dst, send_sem=send, recv_sem=recv, device_id=to, device_id_type=MESH
        )
        c.start()
        sends.append(c)
        return c

    arrivals = {}
    moves = []

    def move(piece, axis, way, half=None):
        o, rx, rz = piece
        at = {"x": rx, "z": rz}
        at[axis] = (at[axis] - way) % 4
        to = SLOT[(o, at["x"], at["z"])]
        frm = SLOT[piece]
        rows = slice(0, PIECE) if half is None else slice(half * 128, half * 128 + 128)
        moves.append(to)
        c = remote(
            w.at[frm, rows], w.at[to, rows], w_send.at[len(moves)], w_recv.at[to, half or 0], side[(axis, way)]
        )
        arrivals.setdefault(to, []).append(c)

    steps = [[] for _ in range(PIECES)]
    for at, piece in enumerate(ORDER):
        o, rx, rz = piece
        first, second = ("x", "z") if o == 0 else ("z", "x")
        r1, r2 = (rx, rz) if o == 0 else (rz, rx)
        out = []
        if r2 == 0:
            if r1 == 0:
                out += [(2, first, 1, None), (2, first, -1, None)]
            elif r1 == 3:
                out += [(0, first, 1, 0)]
            elif r1 == 1:
                out += [(0, first, -1, 1)]
            out += [(3, second, 1, None), (3, second, -1, None)]
        elif r2 == 3:
            out += [(1, second, 1, 0)]
        elif r2 == 1:
            out += [(1, second, -1, 1)]
        for rank, axis, way, half in out:
            step = min(at + HOLD.get((piece, axis, way), 0), PIECES - 1)
            steps[step].append((rank, ORDER_RANK[piece], piece, axis, way, half))

    def pass_on(j):
        for _, _, piece, axis, way, half in sorted(steps[j], key=lambda e: e[:2]):
            move(piece, axis, way, half)

    for c in own_w:
        c.wait()
    other = remote(w.at[0], w.at[SLOT[(1, 0, 0)]], w_send.at[0], w_recv.at[SLOT[(1, 0, 0)], 0], p_yh)
    pass_on(0)

    loads = [
        local_copy(downs_q, dn_cat.at[0:16], 4),
        local_copy(downs_k, dn_cat.at[16:32], 5),
        local_copy(downs_v, dn_cat.at[32:48], 6),
        local_copy(oup, oup_v, 10),
        local_copy(odown, od_v, 11),
        local_copy(saved, sc, 12),
    ]
    for c in loads:
        c.start()

    load_states.wait()

    def squares(c, total):
        at = pl.multiple_of(c * 256, 256)
        one = big[:, pl.ds(at, 128)].astype(jnp.float32)
        two = big[:, pl.ds(at + 128, 128)].astype(jnp.float32)
        return total + (one * one + two * two)

    total = lax.fori_loop(0, 32, squares, jnp.zeros((OWN, 128), jnp.float32))
    factor = lax.rsqrt(jnp.sum(total, axis=1, keepdims=True) / 8192.0 + EPS)

    def source(piece):
        o, rx, rz = piece
        return (((x + rx) % 4) * 2 + (yh + o) % 2) * 4 + (z + rz) % 4

    def columns(g):
        return pl.ds(g * SPAN, SPAN)

    def normed(g):
        for j in range(g * SPAN, (g + 1) * SPAN):
            at = pl.multiple_of(source(ORDER[j]) * PIECE, PIECE)
            wide = big[:, pl.ds(at, PIECE)].astype(jnp.float32)
            scale = gain[pl.ds(at, PIECE)].astype(jnp.float32).reshape(1, PIECE)
            nb[t, j] = (wide * factor * scale).astype(jnp.bfloat16)

    n_mine = {}

    def send_normed(g):
        mine = nb.at[t, columns(g)]
        n_mine[g] = (
            remote(mine, mine, n_send.at[0, g], n_recv.at[0, g], p_yl),
            remote(mine, mine, n_send.at[1, g], n_recv.at[1, g], p_core),
        )

    for g in range(GROUPS):
        normed(g)
        if g < 2:
            send_normed(g)

    exchanges = {}

    def swap(at, src, dst, to):
        exchanges[at] = remote(src, dst, g_send.at[at], g_recv.at[at], to)

    def got(at):
        exchanges[at].wait_recv()

    load_grad = local_copy(grad, big, 13)
    load_grad.start()
    for c in loads[:3]:
        c.wait()

    total = jnp.zeros((OWN, 48), jnp.float32)
    for j in range(PIECES):
        at = pl.multiple_of(source(ORDER[j]) * PIECE, PIECE)
        total = total + f32_dot(nb[t, j], dn_cat[:, pl.ds(at, PIECE)], NT)
    low[t, :, 0:48] = total.astype(jnp.bfloat16)
    low[t, :, 48:128] = jnp.zeros((OWN, 80), jnp.bfloat16)

    up_cat[...] = jnp.zeros_like(up_cat)
    ups = [
        local_copy(up_q, up_cat.at[0:16, 0:1024], 7),
        local_copy(up_k, up_cat.at[16:32, 1024:1152], 8),
        local_copy(up_v, up_cat.at[32:48, 1152:1280], 9),
    ]
    for c in ups:
        c.start()

    lane = lax.broadcasted_iota(jnp.int32, (256, HEAD), 1)
    index = (lane % 64).astype(jnp.float32)
    inverse = jnp.exp(index * (-2.0 * math.log(10000.0) / HEAD))
    sign = jnp.where(lane < 64, -1.0, 1.0).astype(jnp.float32)

    def tables(i, carry):
        at = pl.multiple_of(i * 256, 256)
        position = lax.broadcasted_iota(jnp.int32, (256, HEAD), 0) + (s * BLOCK + at)
        angle = position.astype(jnp.float32) * ROPE_STRETCH * inverse
        cos_t[pl.ds(at, 256), :] = jnp.cos(angle)
        sin_t[pl.ds(at, 256), :] = jnp.sin(angle) * sign
        return carry

    for c in loads[3:]:
        c.wait()
    load_grad.wait()

    u3, u4, u5 = core * 16, core * 16 + yl * 8, core * 16 + yl * 8 + yh * 4
    v3, v4, v5 = (1 - core) * 16, u3 + (1 - yl) * 8, u4 + (1 - yh) * 4
    d5, e5 = yh * 4, (1 - yh) * 4
    theirs = (1 - yl) * 2 + core

    def g0():
        total = jnp.zeros((16, OWN), jnp.float32)
        for c in range(16):
            cols = slice(c * 512, c * 512 + 512)
            total = total + f32_dot(oup_v[:, cols], big[:, cols], NT)
        lg[t] = total.astype(jnp.bfloat16)
        for b in range(4):
            part[b] = f32_dot(od_v[...], sc[b * 256 : b * 256 + 256, :], NT)
        swap(0, part.at[pl.ds((1 - yl) * 2, 2)], part_r1, p_yl)
        swap(1, lg.at[t], lg.at[t], p_yl)
        swap(2, lg.at[t], lg.at[t], p_core)

    def send_low():
        swap(3, low.at[t], low.at[t], p_yl)
        swap(4, low.at[t], low.at[t], p_core)

    def g1():
        got(0)
        keep = pl.ds(yl * 2, 2)
        part[keep] = part[keep] + part_r1[...]
        swap(5, part.at[yl * 2 + 1 - core], part_r2, p_core)
        got(1)
        swap(6, lg.at[theirs], lg.at[theirs], p_core)
        got(3)
        swap(7, low.at[theirs], low.at[theirs], p_core)

    def g2():
        got(5)
        ctx[...] = (part[t] + part_r2[...]).astype(jnp.bfloat16)
        for b in range(32):
            up[b] = ADAPTER_SCALE * f32_dot(ctx[...], big[:, b * 256 : b * 256 + 256])
        swap(8, up.at[pl.ds(v3, 16)], up_r3, p_core)
        got(2)
        got(6)
        for b in range(8):
            sums = jnp.zeros((16, 128), jnp.float32)
            for k in range(4):
                sums = sums + f32_dot(lg[k], sc[k * 256 : k * 256 + 256, b * 128 : b * 128 + 128])
            dn[b] = ADAPTER_SCALE * sums

    def g3():
        got(8)
        up[pl.ds(u3, 16)] = up[pl.ds(u3, 16)] + up_r3[...]
        swap(9, up.at[pl.ds(v4, 8)], up_r4, p_yl)

    def g4():
        got(9)
        up[pl.ds(u4, 8)] = up[pl.ds(u4, 8)] + up_r4[...]
        swap(10, up.at[pl.ds(v5, 4)], up_r5, p_yh)
        swap(11, dn.at[pl.ds(e5, 4)], dn_r5, p_yh)

    def g5():
        got(10)
        got(11)
        up[pl.ds(u5, 4)] = up[pl.ds(u5, 4)] + up_r5[...]
        dn[pl.ds(d5, 4)] = dn[pl.ds(d5, 4)] + dn_r5[...]
        for k in range(3):
            there = (x + k + 1) % 4
            swap(12 + k, up.at[u5 + there], up_rx.at[k], x_others[k])
            swap(15 + k, dn.at[d5 + there], dn_rx.at[k], x_others[k])

    def g6():
        for k in range(6):
            got(12 + k)
        up_rz[z] = up[u5 + x] + up_rx[0] + up_rx[1] + up_rx[2]
        dn_rz[z] = dn[d5 + x] + dn_rx[0] + dn_rx[1] + dn_rx[2]
        for k in range(3):
            swap(18 + k, up_rz.at[z], up_rz.at[z], z_others[k])
            swap(21 + k, dn_rz.at[z], dn_rz.at[z], z_others[k])

    def g7():
        for k in range(6):
            got(18 + k)
        up_g[u5 + x] = up_rz[0] + up_rz[1] + up_rz[2] + up_rz[3]
        dn_g[d5 + x] = dn_rz[0] + dn_rz[1] + dn_rz[2] + dn_rz[3]
        for k in range(3):
            swap(24 + k, up_g.at[u5 + x], up_g.at[u5 + x], x_others[k])
            swap(27 + k, dn_g.at[d5 + x], dn_g.at[d5 + x], x_others[k])

    def g8():
        for k in range(6):
            got(24 + k)
        swap(30, up_g.at[pl.ds(u5, 4)], up_g.at[pl.ds(u5, 4)], p_yh)
        swap(31, dn_g.at[pl.ds(d5, 4)], dn_g.at[pl.ds(d5, 4)], p_yh)

    def g9():
        got(30)
        swap(32, up_g.at[pl.ds(u4, 8)], up_g.at[pl.ds(u4, 8)], p_yl)
        got(31)
        for b in range(8):
            dgrad[:, b * 128 : b * 128 + 128] = dn_g[b]

    def g10():
        got(32)
        swap(33, up_g.at[pl.ds(u3, 16)], up_g.at[pl.ds(u3, 16)], p_core)

    def g11():
        got(33)
        for b in range(32):
            ugrad[:, b * 256 : b * 256 + 256] = up_g[b]

    def adapter():
        got(4)
        got(7)
        for c in ups:
            c.wait()

        def rows_of(i, carry):
            rows = pl.ds(pl.multiple_of(i * 256, 256), 256)
            for c in range(5):
                cols = slice(c * 256, c * 256 + 256)
                acc[rows, cols] = ADAPTER_SCALE * f32_dot(low[i], up_cat[:, cols])
            return carry

        lax.fori_loop(0, 4, rows_of, 0)

    def multiply(groups, tiles):
        blocks = [j for g in groups for j in range(g * SPAN, (g + 1) * SPAN)]

        def rows_of(i, carry):
            rows = pl.ds(pl.multiple_of(i * 256, 256), 256)
            for c in tiles:
                cols = slice(c * 256, c * 256 + 256)
                total = f32_dot(nb[i, blocks[0]], w[blocks[0], :, cols])
                for j in blocks[1:]:
                    total = total + f32_dot(nb[i, j], w[j, :, cols])
                acc[rows, cols] += total
            return carry

        lax.fori_loop(0, 4, rows_of, 0)

    passed = []

    def meet(g):
        n_mine[g][0].wait_recv()
        there = nb.at[theirs, columns(g)]
        fwd = remote(there, there, n_send.at[2, g], n_recv.at[2, g], p_core)
        passed.append((g, fwd))

    def ready():
        g, fwd = passed.pop(0)
        n_mine[g][1].wait_recv()
        fwd.wait_recv()
        return g

    g0()
    send_low()
    for g in range(2, FIRST):
        send_normed(g)

    hooks = {
        3: [lambda: lax.fori_loop(0, 4, tables, 0)],
        6: [g1],
        8: [g2, adapter],
        9: [g3],
        14: [g4],
        18: [g5],
        28: [g6],
    }
    arrivals[SLOT[(1, 0, 0)]] = [other]
    sent = FIRST
    for j in range(PIECES):
        if j > 0:
            for c in arrivals[j]:
                c.wait_recv()
            pass_on(j)
        if j % 2 == 0 and j > 0 and sent < GROUPS:
            send_normed(sent)
            sent += 1
        for f in hooks.get(j, []):
            f()
        for g in range(GROUPS):
            if MEET[g] == j:
                meet(g)
                if len(passed) > 1 and j < PIECES - 1:
                    multiply([ready()], range(5))
    last = [ready() for _ in range(len(passed))]
    multiply(last, [4])

    def rotated(value, rows):
        return value * cos_t[rows, :] + pltpu.roll(value, 64, 1) * sin_t[rows, :]

    def keys_of(i, carry):
        rows = pl.ds(pl.multiple_of(i * 256, 256), 256)
        k_own[rows, :] = rotated(acc[rows, 1024:1152], rows).astype(jnp.bfloat16)
        v_own[rows, 0:128] = acc[rows, 1152:1280].astype(jnp.bfloat16)
        return carry

    lax.fori_loop(0, 4, keys_of, 0)
    swap(34, k_own, k_prior, later)
    swap(35, v_own.at[:, 0:128], v_prior.at[:, 0:128], later)

    to_exponent = math.log2(math.e) / math.sqrt(HEAD)

    g7()
    multiply(last, range(4))

    def turn(h):
        cols = pl.ds(pl.multiple_of(h * HEAD, HEAD), HEAD)
        for i in range(4):
            rows = slice(i * 256, i * 256 + 256)
            q_v[rows, cols] = (rotated(acc[rows, cols], rows) * to_exponent).astype(jnp.bfloat16)

    bias = jnp.where(flag[0] == 1, 0.0, -1e30).astype(jnp.float32)
    key = lax.broadcasted_iota(jnp.int32, (256, 256), 1)
    query = lax.broadcasted_iota(jnp.int32, (256, 256), 0)
    place = lax.broadcasted_iota(jnp.int32, (256, HEAD), 1)
    wide_place = lax.broadcasted_iota(jnp.int32, (512, HEAD), 1)

    def own_keys(h, carry):
        turn(jnp.minimum(h + 1, HEADS - 1))
        cols = pl.ds(pl.multiple_of(h * HEAD, HEAD), HEAD)

        def scores_of(i):
            return f32_dot(q_v[i * 256 : i * 256 + 256, cols], k_own[0 : i * 256 + 256, :], NT)

        later_scores = scores_of(3)
        for i in (3, 2, 1, 0):
            rows = slice(i * 256, i * 256 + 256)
            scores = later_scores
            if i > 0:
                later_scores = scores_of(i - 1)
            corner = jnp.where(key <= query, scores[:, i * 256 :], -jnp.inf)
            scores = jnp.concatenate([scores[:, : i * 256], corner], axis=1) if i > 0 else corner
            summit = jnp.max(scores, axis=1, keepdims=True)
            raised = jnp.exp2(scores - summit).astype(jnp.bfloat16)
            found = f32_dot(raised, v_own[0 : i * 256 + 256, :])
            acc[rows, cols] = found[:, 0:128]
            acc[rows, 1024:1152] = jnp.where(place == h, found[:, 128:256], acc[rows, 1024:1152])
            acc[rows, 1152:1280] = jnp.where(place == h, summit, acc[rows, 1152:1280])
        return carry

    def prior_keys(h, carry):
        cols = pl.ds(pl.multiple_of(h * HEAD, HEAD), HEAD)

        def scores_of(i):
            return f32_dot(q_v[i * 512 : i * 512 + 512, cols], k_prior[...], NT)

        later_scores = scores_of(0)
        for i in range(2):
            rows = slice(i * 512, i * 512 + 512)
            scores = later_scores
            if i == 0:
                later_scores = scores_of(1)
            norm = jnp.sum(jnp.where(wide_place == h, acc[rows, 1024:1152], 0.0), axis=1, keepdims=True)
            before = jnp.max(jnp.where(wide_place == h, acc[rows, 1152:1280], -jnp.inf), axis=1, keepdims=True)
            summit = jnp.maximum(before, jnp.max(scores, axis=1, keepdims=True) + bias)
            raised = jnp.exp2(scores - (summit - bias)).astype(jnp.bfloat16)
            found = f32_dot(raised, v_prior[...])
            shrink = jnp.exp2(before - summit)
            total = acc[rows, cols] * shrink + found[:, 0:128]
            norm = norm * shrink + found[:, 128:256]
            sc[rows, cols] = (total / norm).astype(jnp.bfloat16)
        return carry

    turn(0)
    lax.fori_loop(0, 4, own_keys, 0)
    g8()
    lax.fori_loop(4, 8, own_keys, 0)
    g9()
    got(34)
    got(35)
    stores = []

    def finish(first, stop):
        lax.fori_loop(first, stop, prior_keys, 0)
        cols = slice(first * HEAD, stop * HEAD)
        stores.append(pltpu.make_async_copy(sc.at[:, cols], context.at[:, cols], local.at[14 + len(stores)]))
        stores[-1].start()

    finish(0, 4)
    g10()
    finish(4, 6)
    g11()
    finish(6, 8)
    for c in stores:
        c.wait()
    for c in sends:
        c.wait_send()


def hand_over(context, dgrad, ugrad, context_out, dgrad_out, ugrad_out, done):
    copies = [(context.at[pl.ds(i * 128, 128)], context_out.at[pl.ds(i * 128, 128)]) for i in range(8)]
    copies += [(ugrad, ugrad_out), (dgrad, dgrad_out)]
    started = [pltpu.make_async_copy(src, dst, done.at[i]) for i, (src, dst) in enumerate(copies)]
    for c in started:
        c.start()
    for c in started:
        c.wait()


def on_device(
    states_forward, norm_gain, query_weight, frozen_key_weight, frozen_value_weight, query_down, query_up,
    key_down_matrix, key_up_matrix, value_down_matrix, value_up_matrix, shifted, saved_context, output_gradient,
    out_down, out_up,
):
    bf16, f32 = jnp.bfloat16, jnp.float32
    hbm = pl.BlockSpec(memory_space=pl.ANY)
    vmem = pl.BlockSpec(memory_space=pltpu.VMEM)
    scratch = [
        pltpu.VMEM((PIECES, PIECE, COLS), bf16),
        pltpu.VMEM((4, PIECES, OWN, PIECE), bf16),
        pltpu.VMEM((BLOCK, COLS), f32),
        pltpu.VMEM((OWN, 8192), bf16),
        pltpu.VMEM((BLOCK, 1024), bf16),
        pltpu.VMEM((48, 8192), bf16),
        pltpu.VMEM((128, COLS), bf16),
        pltpu.VMEM((4, OWN, 128), bf16),
        pltpu.VMEM((BLOCK, HEAD), f32),
        pltpu.VMEM((BLOCK, HEAD), f32),
        pltpu.VMEM((16, 8192), bf16),
        pltpu.VMEM((16, 1024), bf16),
        pltpu.VMEM((4, 16, OWN), bf16),
        pltpu.VMEM((4, 16, OWN), f32),
        pltpu.VMEM((2, 16, OWN), f32),
        pltpu.VMEM((16, OWN), f32),
        pltpu.VMEM((16, OWN), bf16),
        pltpu.VMEM((32, 16, 256), f32),
        pltpu.VMEM((16, 16, 256), f32),
        pltpu.VMEM((8, 16, 256), f32),
        pltpu.VMEM((4, 16, 256), f32),
        pltpu.VMEM((3, 16, 256), f32),
        pltpu.VMEM((4, 16, 256), f32),
        pltpu.VMEM((8, 16, 128), f32),
        pltpu.VMEM((4, 16, 128), f32),
        pltpu.VMEM((3, 16, 128), f32),
        pltpu.VMEM((4, 16, 128), f32),
        pltpu.VMEM((32, 16, 256), f32),
        pltpu.VMEM((8, 16, 128), f32),
        pltpu.VMEM((BLOCK, 1024), bf16),
        pltpu.VMEM((BLOCK, HEAD), bf16),
        pltpu.VMEM((BLOCK, 2 * HEAD), bf16),
        pltpu.VMEM((BLOCK, HEAD), bf16),
        pltpu.VMEM((BLOCK, 2 * HEAD), bf16),
        pltpu.SemaphoreType.DMA((18,)),
        pltpu.SemaphoreType.DMA((41,)),
        pltpu.SemaphoreType.DMA((PIECES, 2)),
        pltpu.SemaphoreType.DMA((3, GROUPS)),
        pltpu.SemaphoreType.DMA((3, GROUPS)),
        pltpu.SemaphoreType.DMA((36,)),
        pltpu.SemaphoreType.DMA((36,)),
    ]
    station = lax.axis_index("seq")
    flag = ((station - shifted) % 2).astype(jnp.int32)
    context, down_t, up_t = pl.pallas_call(
        project,
        out_shape=(
            jax.ShapeDtypeStruct((BLOCK, 1024), bf16),
            jax.ShapeDtypeStruct((16, 1024), f32),
            jax.ShapeDtypeStruct((16, 8192), f32),
        ),
        in_specs=[pl.BlockSpec(memory_space=pltpu.SMEM), hbm, vmem] + [hbm] * 13,
        out_specs=(hbm, vmem, vmem),
        scratch_shapes=scratch,
        compiler_params=pltpu.CompilerParams(
            collective_id=0, has_side_effects=True, vmem_limit_bytes=64 * 1024 * 1024
        ),
        name="fused",
    )(
        flag, states_forward, norm_gain, query_weight, frozen_key_weight, frozen_value_weight,
        query_down.T, key_down_matrix.T, value_down_matrix.T, query_up, key_up_matrix, value_up_matrix,
        saved_context, output_gradient, out_down.T, out_up,
    )
    return context, down_t.T, up_t


def solution(mesh):
    placed = (
        P(("seq", "tensor"), None),
        P(),
        P("seq", "tensor"),
        P("seq", "tensor"),
        P("seq", "tensor"),
        P(),
        P(None, "tensor"),
        P(),
        P(None, "tensor"),
        P(),
        P(None, "tensor"),
        P("tensor"),
        P("seq", "tensor"),
        P(("seq", "tensor"), None),
        P("tensor", None),
        P(),
    )
    return jax.shard_map(
        on_device,
        mesh=mesh,
        in_specs=placed,
        out_specs=(P("seq", "tensor"), P("tensor", None), P()),
        check_vma=False,
    )
```
